32 devices in a mesh: ctx: 8 (over y, x, core), tp: 4 (over z).
Axes of the slice: x: 2, y: 2, z: 4, core: 2. Of those that a mesh axis runs over, the one named last changes fastest.
Arguments:
- inputs: bfloat16 [1024, 2048], P('ctx', 'tp'), may hold values from -6 to 6
- residue: float32 [2048, 16], P('tp'), may hold values from -1.5 to 1.5
- log_rate: float32 [2048, 16], P('tp'), may hold values from -1 to 6.5
- skip: float32 [2048], P('tp'), may hold values from 0.5 to 1.5
- out_weight: bfloat16 [2048, 8192], P('tp'), may hold values from -0.125 to 0.125
- out_grad: bfloat16 [1024, 8192], P(('ctx', 'tp')), may hold values from -6 to 6
Outputs:
- out: bfloat16 [1024, 8192], P(('ctx', 'tp'))
- grad_input: bfloat16 [1024, 2048], P('ctx', 'tp')
- grad_residue: float32 [2048, 16], P('tp')
- grad_log_rate: float32 [2048, 16], P('tp')
- grad_skip: float32 [2048], P('tp')
The draws below stay inside these ranges and needn't reach their ends.
All inputs are finite; a program needn't handle non-finite values.
Results may differ from the reference program's by a relative error of at most 0.02.
Values may be sent and summed in bfloat16 or wider, within the bound.
No kernel may reach another device: no remote copies, remote signals or barrier semaphores. Data moves between devices by JAX's collectives and lax.ppermute only.
A program may use at most 128 MiB of HBM per device.

```python
import math
import jax
import jax.numpy as jnp
from jax import lax

CH_DEV = 512
DIM = 8192
MODES = 16
SEQ = 1024
CHANNELS = 2048


def draw_log_rate(key, part):
    key = jax.random.fold_in(key, 7)
    first = jax.random.fold_in(key, 0)
    return jax.random.uniform(first, (CHANNELS, MODES), jnp.float32, -1.0, 6.5)


def block_scale(own_key, shape, shards, smallest, high):
    def one(axis_at, parts):
        steps = jax.random.uniform(jax.random.fold_in(jax.random.fold_in(own_key, 6), axis_at), (parts,), jnp.float32, smallest / len(shards), high / len(shards))
        return jnp.repeat(jnp.exp(steps), shape[axis_at] // parts).reshape((-1,) + (1,) * (len(shape) - axis_at - 1))

    factor_of = one(*shards[0])
    for cut in shards[1:]:
        factor_of = factor_of * one(*cut)
    return factor_of


def normal_values(key, shape, scale, most, shards=(), held_as=jnp.bfloat16):
    values = scale * jax.random.normal(key, shape, jnp.float32)
    if shards:
        values = values * block_scale(key, shape, shards, -0.22, 0.18)
    return jnp.clip(values, -most, most).astype(held_as)


def setup_inputs(seed: int = 0) -> dict:
    key_of = jax.random.split(jax.random.key(seed), 7)
    inputs = normal_values(key_of[0], (SEQ, CHANNELS), 1.0, 6.0, ((0, 8), (1, 4)))
    residue = normal_values(key_of[1], (CHANNELS, MODES), 0.25, 1.5, ((0, 4),), jnp.float32)
    log_rate = draw_log_rate(jax.random.fold_in(key_of[6], 71), 0)
    skip = jnp.clip(1.0 + 0.1 * jax.random.normal(key_of[3], (CHANNELS,), jnp.float32), 0.5, 1.5)
    out_weight = normal_values(key_of[4], (CHANNELS, DIM), CHANNELS ** -0.5, 0.125, ((0, 4),))
    out_grad = normal_values(key_of[5], (SEQ, DIM), 1.0, 6.0, ((0, 32),))
    return {"inputs": inputs, "residue": residue, "log_rate": log_rate, "skip": skip, "out_weight": out_weight, "out_grad": out_grad}


def reference(inputs, residue, log_rate, skip, out_weight, out_grad):
    x = inputs.astype(jnp.float32)
    places = jnp.arange(SEQ).astype(jnp.float32)
    rate = jnp.exp(log_rate) / SEQ
    filt = jnp.zeros(x.shape, jnp.float32)
    for mode in range(MODES):
        rate_n = rate[:, mode][None, :]
        basis_n = jnp.sqrt(2.0 * rate_n) * jnp.exp(-(rate_n * places[:, None]))
        filt = filt + residue[:, mode][None, :] * basis_n
    length = 2 * SEQ
    spec_x = jnp.fft.rfft(x, n=length, axis=0)
    spec_f = jnp.fft.rfft(filt, n=length, axis=0)
    conv = jnp.fft.irfft(spec_x * spec_f, n=length, axis=0)[:SEQ]
    merged = (conv + skip[None, :] * x).astype(jnp.bfloat16)
    total = jnp.zeros((SEQ, DIM), jnp.float32)
    for group in range(CHANNELS // CH_DEV):
        block = merged[:, group * CH_DEV:(group + 1) * CH_DEV]
        weights = out_weight[group * CH_DEV:(group + 1) * CH_DEV]
        partial_sum = jnp.dot(block, weights, preferred_element_type=jnp.float32).astype(jnp.bfloat16)
        total = total + lax.optimization_barrier(partial_sum).astype(jnp.float32)
    out = total.astype(jnp.bfloat16)
    grad_merged = lax.dot_general(out_grad, out_weight, (((1,), (1,)), ((), ())), preferred_element_type=jnp.float32).astype(jnp.bfloat16)
    g = grad_merged.astype(jnp.float32)
    spec_g = jnp.fft.rfft(g, n=length, axis=0)
    back_conv = jnp.fft.irfft(spec_g * jnp.conj(spec_f), n=length, axis=0)[:SEQ]
    grad_input = (back_conv + skip[None, :] * g).astype(jnp.bfloat16)
    filt_grad = jnp.fft.irfft(spec_g * jnp.conj(spec_x), n=length, axis=0)[:SEQ]
    res_cols = []
    log_cols = []
    for mode in range(MODES):
        rate_n = rate[:, mode][None, :]
        basis_n = jnp.sqrt(2.0 * rate_n) * jnp.exp(-(rate_n * places[:, None]))
        weighted = filt_grad * basis_n
        res_cols.append(lax.optimization_barrier(jnp.sum(weighted, axis=0)))
        log_cols.append(lax.optimization_barrier(jnp.sum(weighted * residue[:, mode][None, :] * (0.5 - rate_n * places[:, None]), axis=0)))
    scale = math.sqrt(SEQ)
    grad_residue = jnp.stack(res_cols, axis=1) / scale
    grad_log_rate = jnp.stack(log_cols, axis=1) / scale
    grad_skip = lax.optimization_barrier(jnp.sum(g * x, axis=0)) / scale
    return (out, grad_input, grad_residue, grad_log_rate, grad_skip)
```

```python
import functools
import math

import jax
import jax.numpy as jnp
from jax import lax
from jax.experimental import pallas as pl
from jax.experimental.pallas import tpu as pltpu
from jax.sharding import PartitionSpec as P

F32 = jnp.float32
BF16 = jnp.bfloat16
STEP = 8
CLEAR_FLOPS = 4_000_000_000
HALVES = 2


def call(body, outs, scratch, args, flops=1024):
    whole = pl.BlockSpec(memory_space=pltpu.VMEM)
    return pl.pallas_call(
        body,
        out_shape=outs,
        in_specs=[whole] * len(args),
        out_specs=[whole] * len(outs),
        scratch_shapes=scratch,
        compiler_params=pltpu.CompilerParams(vmem_limit_bytes=12 << 20),
        cost_estimate=pl.CostEstimate(flops=flops, bytes_accessed=1024, transcendentals=0),
    )(*args)


def row_of(ref, at, like):
    return jnp.broadcast_to(ref[pl.ds(at, 1), :], like.shape)


def part_of(ref, which, modes):
    return ref[pl.ds(which * modes, modes), :]


def clear_body(state_ref):
    state_ref[...] = jnp.zeros_like(state_ref)


def ends_body(seq, x_ref, log_ref, zero_ref, x_f, rate_ref, ends_ref):
    tok = x_ref.shape[0]
    modes = log_ref.shape[0]
    rate = jnp.exp(log_ref[...]) / seq
    a = jnp.exp(-rate)
    rate_ref[...] = rate
    x_f[...] = x_ref[...].astype(F32)

    def steps(block, carry):
        h, q = carry
        for inner in range(STEP):
            ah = a * h
            q = a * q + ah
            h = ah + row_of(x_f, block * STEP + inner, a)
        return h, q

    h, q = lax.fori_loop(0, tok // STEP, steps, (zero_ref[...], zero_ref[...]))
    ends_ref[pl.ds(0, modes), :] = h
    ends_ref[pl.ds(modes, modes), :] = q


def table_body(rate_ref, res_ref, skip_ref, table_ref):
    modes = rate_ref.shape[0]
    rate = rate_ref[...]
    norm = jnp.sqrt(2.0 * rate)
    table_ref[pl.ds(0, modes), :] = rate
    table_ref[pl.ds(modes, modes), :] = norm
    table_ref[pl.ds(2 * modes, modes), :] = res_ref[...] * norm
    table_ref[pl.ds(3 * modes, 8), :] = jnp.broadcast_to(skip_ref[...], (8, rate.shape[1]))


def advance(h, q, a_span, span):
    return a_span * h, a_span * (q + span * h)


def pair_ends_body(tok, modes, rate_ref, own_ref, other_ref, pair_ref):
    second = lax.axis_index("ctx") % 2 == 1
    a_chunk = jnp.exp(-(rate_ref[...] * tok))
    own = part_of(own_ref, 0, modes), part_of(own_ref, 1, modes)
    other = part_of(other_ref, 0, modes), part_of(other_ref, 1, modes)
    early = [jnp.where(second, theirs, ours) for ours, theirs in zip(own, other)]
    late = [jnp.where(second, ours, theirs) for ours, theirs in zip(own, other)]
    h, q = advance(*early, a_chunk, tok)
    pair_ref[pl.ds(0, modes), :] = (h + late[0]).astype(BF16)
    pair_ref[pl.ds(modes, modes), :] = (q + late[1]).astype(BF16)


def merged_body(modes, x_f, table_ref, other_ref, *refs):
    *far_refs, merged_ref, start_ref, y_f = refs
    tok = x_f.shape[0]
    rate = part_of(table_ref, 0, modes)
    c = part_of(table_ref, 2, modes)
    a = jnp.exp(-rate)
    a_chunk = jnp.exp(-(rate * tok))
    index = lax.axis_index("ctx")
    pair = index // 2
    h = jnp.zeros_like(a)
    q = jnp.zeros_like(a)
    for j, far in enumerate(far_refs, 1):
        apart = pair - (pair ^ j)
        since = (jnp.maximum(apart - 1, 0) * (2 * tok)).astype(F32)
        far_h, far_q = part_of(far, 0, modes).astype(F32), part_of(far, 1, modes).astype(F32)
        far_h, far_q = advance(far_h, far_q, jnp.exp(-(rate * since)), since)
        h = h + jnp.where(apart > 0, far_h, 0.0)
        q = q + jnp.where(apart > 0, far_q, 0.0)
    h_late, q_late = advance(h, q, a_chunk, tok)
    second = index % 2 == 1
    h = jnp.where(second, h_late + part_of(other_ref, 0, modes), h)
    q = jnp.where(second, q_late + part_of(other_ref, 1, modes), q)
    start_ref[pl.ds(0, modes), :] = h
    start_ref[pl.ds(modes, modes), :] = q

    def steps(block, h):
        for inner in range(STEP):
            at = block * STEP + inner
            h = a * h + row_of(x_f, at, a)
            y_f[pl.ds(at, 1), :] = jnp.sum(c * h, axis=0, keepdims=True)
        return h

    lax.fori_loop(0, tok // STEP, steps, h)
    merged_ref[...] = (y_f[...] + table_ref[pl.ds(3 * modes, 1), :] * x_f[...]).astype(BF16)


def states_body(modes, x_f, table_ref, start_ref, h_ref, q_ref):
    tok = x_f.shape[0]
    a = jnp.exp(-part_of(table_ref, 0, modes))

    def steps(block, carry):
        h, q = carry
        for inner in range(STEP):
            at = block * STEP + inner
            ah = a * h
            q = a * q + ah
            h = ah + row_of(x_f, at, a)
            to = pl.ds(pl.multiple_of(at * modes, 8), modes)
            h_ref[to, :] = h
            q_ref[to, :] = q
        return h, q

    lax.fori_loop(0, tok // STEP, steps, (part_of(start_ref, 0, modes), part_of(start_ref, 1, modes)))


def grads_body(modes, rows, places_of, x_f, table_ref, h_ref, q_ref, *refs):
    *g_refs, g_f, sums_ref = refs
    tok = x_f.shape[0]
    rate = part_of(table_ref, 0, modes)
    a = jnp.exp(-rate)
    places = places_of()
    slot = 0
    for g_ref in g_refs:
        for at in range(g_ref.shape[0] // rows):
            to = pl.multiple_of(places[slot] * rows, 8)
            g_f[pl.ds(to, rows), :] = g_ref[pl.ds(at * rows, rows), :].astype(BF16).astype(F32)
            slot += 1

    def steps(block, carry):
        power, back, by_res, by_rate = carry
        for inner in range(STEP):
            at = block * STEP + inner
            g = row_of(g_f, at, a)
            to = pl.ds(pl.multiple_of(at * modes, 8), modes)
            back = back + power * g
            power = power * a
            by_res = by_res + g * h_ref[to, :]
            by_rate = by_rate + g * q_ref[to, :]
        return power, back, by_res, by_rate

    zero = jnp.zeros_like(a)
    _, back, by_res, by_rate = lax.fori_loop(0, tok // STEP, steps, (jnp.ones_like(a), zero, zero, zero))
    sums_ref[pl.ds(0, modes), :] = back
    sums_ref[pl.ds(modes, modes), :] = by_res
    sums_ref[pl.ds(2 * modes, modes), :] = 0.5 * by_res - rate * by_rate
    direct = jnp.sum(g_f[...] * x_f[...], axis=0, keepdims=True)
    sums_ref[pl.ds(3 * modes, 8), :] = jnp.broadcast_to(direct, (8, direct.shape[1]))


def pair_sums_body(tok, modes, table_ref, own_ref, other_ref, pair_ref):
    second = lax.axis_index("ctx") % 2 == 1
    a_chunk = jnp.exp(-(part_of(table_ref, 0, modes) * tok))
    own = part_of(own_ref, 0, modes)
    other = part_of(other_ref, 0, modes)
    early = jnp.where(second, other, own)
    late = jnp.where(second, own, other)
    pair_ref[pl.ds(0, modes), :] = (early + a_chunk * late).astype(BF16)
    both = pl.ds(modes, 2 * modes)
    pair_ref[both, :] = (own_ref[both, :] + other_ref[both, :]).astype(BF16)
    direct = own_ref[pl.ds(3 * modes, 1), :] + other_ref[pl.ds(3 * modes, 1), :]
    pair_ref[pl.ds(3 * modes, modes), :] = jnp.broadcast_to(direct, own.shape).astype(BF16)


def input_body(seq, modes, g_f, table_ref, other_ref, pair_ref, *refs):
    *far_refs, grad_ref, by_res_ref, by_log_ref, by_skip_ref, y_f = refs
    tok = g_f.shape[0]
    rate = part_of(table_ref, 0, modes)
    norm = part_of(table_ref, 1, modes)
    c = part_of(table_ref, 2, modes)
    a = jnp.exp(-rate)
    a_chunk = jnp.exp(-(rate * tok))
    index = lax.axis_index("ctx")
    pair = index // 2
    z = jnp.zeros_like(a)
    for j, far in enumerate(far_refs, 1):
        apart = (pair ^ j) - pair
        until = (jnp.maximum(apart - 1, 0) * (2 * tok)).astype(F32)
        decay = jnp.exp(-(rate * until))
        z = z + jnp.where(apart > 0, decay * far[pl.ds(0, modes), :].astype(F32), 0.0)
    z = jnp.where(index % 2 == 0, a_chunk * z + part_of(other_ref, 0, modes), z)

    def steps(block, z):
        for inner in range(STEP):
            at = tok - 1 - (block * STEP + inner)
            z = a * z + row_of(g_f, at, a)
            y_f[pl.ds(at, 1), :] = jnp.sum(c * z, axis=0, keepdims=True)
        return z

    lax.fori_loop(0, tok // STEP, steps, z)
    grad_ref[...] = (y_f[...] + table_ref[pl.ds(3 * modes, 1), :] * g_f[...]).astype(BF16)
    rest = pl.ds(modes, 3 * modes)
    total = pair_ref[rest, :].astype(F32)
    for far in far_refs:
        total = total + far[rest, :].astype(F32)
    scale = 1.0 / math.sqrt(seq)
    by_res_ref[...] = scale * (norm * total[:modes])
    by_log_ref[...] = scale * (c * total[modes:2 * modes])
    by_skip_ref[...] = scale * total[2 * modes:2 * modes + 1]


def from_other_core(array, blocks):
    return lax.ppermute(array, "ctx", [(i, i ^ 1) for i in range(blocks)])


def from_pairs(array, blocks):
    return [lax.ppermute(array, "ctx", [(i, i ^ (2 * j)) for i in range(blocks)]) for j in range(1, blocks // 2)]


def outer(array):
    return lax.ppermute(array, "tp", [(0, 1), (1, 0), (2, 3), (3, 2)])


def inner(array):
    return lax.ppermute(array, "tp", [(1, 2), (2, 1), (0, 0), (3, 3)])


def back_dot(rows_in, weight):
    return lax.dot_general(rows_in, weight, (((1,), (1,)), ((), ())), preferred_element_type=F32)


def at_end():
    index = lax.axis_index("tp")
    return (index == 0) | (index == 3)


def inward(far):
    low = lax.axis_index("tp") < 2
    return jnp.where(low, 3, 0) if far else jnp.where(low, 2, 1)


def share_body(span, merged_ref, weight_ref, share_ref):
    cut = share_ref.shape[1]
    tile = min(cut, 512)
    merged = merged_ref[...]
    for at in range(0, cut, tile):
        weight = weight_ref[:, span.start + at:span.start + at + tile]
        share_ref[:, at:at + tile] = jnp.dot(merged, weight, preferred_element_type=F32).astype(BF16)


def share_rows(share_ref, at, rows):
    return share_ref[pl.ds(pl.multiple_of(at * rows, 16), rows), :]


def send_body(span, far, share_ref, passing_ref, out_ref):
    rows = out_ref.shape[0]
    end = at_end()

    @pl.when(end)
    def _():
        out_ref[...] = share_rows(share_ref, inward(far), rows)

    @pl.when(jnp.logical_not(end))
    def _():
        out_ref[...] = passing_ref[:, span]


def back_tiles(rows_ref, weight_ref, start):
    width = rows_ref.shape[1]
    tile = min(width, 1024)
    total = None
    for at in range(0, width, tile):
        part = back_dot(rows_ref[:, at:at + tile], weight_ref[:, start + at:start + at + tile])
        total = part if total is None else total + part
    return total


def near_body(own_ref, beside_ref, weight_ref, g_ref, rows_ref):
    rows = own_ref.shape[0]
    rows_ref[pl.ds(0, rows), :] = own_ref[...]
    rows_ref[pl.ds(rows, rows), :] = beside_ref[...]
    g_ref[...] = back_tiles(rows_ref, weight_ref, 0)


def far_body(span, second_ref, third_ref, across_ref, far_ref, weight_ref, *refs):
    *before_refs, g_ref, rows_ref = refs
    rows = second_ref.shape[0]
    end = at_end()

    @pl.when(end)
    def _():
        rows_ref[pl.ds(0, rows), :] = second_ref[...]
        rows_ref[pl.ds(rows, rows), :] = third_ref[...]

    @pl.when(jnp.logical_not(end))
    def _():
        rows_ref[pl.ds(0, rows), :] = across_ref[:, span]
        rows_ref[pl.ds(rows, rows), :] = far_ref[...]

    total = back_tiles(rows_ref, weight_ref, span.start)
    for before in before_refs:
        total = total + before[...]
    g_ref[...] = total


def add_body(far, share_ref, got_ref, out_ref):
    rows = out_ref.shape[0]
    block = share_rows(share_ref, inward(far), rows).astype(F32)
    out_ref[...] = (block + got_ref[...].astype(F32)).astype(BF16)


def add_whole_body(spans, *refs):
    *in_refs, out_ref = refs
    rows = out_ref.shape[0]
    for at, span in enumerate(spans):
        share_ref, got_ref = in_refs[2 * at:2 * at + 2]
        block = share_rows(share_ref, inward(False), rows).astype(F32)
        out_ref[:, span] = (block + got_ref[...].astype(F32)).astype(BF16)


def last_body(spans, *refs):
    *done_refs, share_ref, got_ref, out_ref = refs
    rows = share_ref.shape[0] // 4
    end = at_end()
    for done_ref, span in zip(done_refs, spans):
        out_ref[:, span] = done_ref[...]
    block = share_rows(share_ref, lax.axis_index("tp") ^ 1, rows).astype(F32)
    out_ref[:, spans[-1]] = (block + jnp.where(end, 0.0, got_ref[...].astype(F32))).astype(BF16)


def total_body(spans, *refs):
    *share_refs, last_ref, near_ref, out_ref = refs
    rows = out_ref.shape[0]
    end = at_end()
    for share_ref, span in zip(share_refs, spans):
        total = share_rows(share_ref, lax.axis_index("tp"), rows).astype(F32) + last_ref[:, span].astype(F32)
        out_ref[:, span] = (total + jnp.where(end, 0.0, near_ref[:, span].astype(F32))).astype(BF16)


def line_of_four(out_grad, out_weight, merged, x_f, states_of, grads_of):
    rows, width = out_grad.shape
    cut = width // HALVES
    spans = [slice(at * cut, (at + 1) * cut) for at in range(HALVES)]
    piece = [jax.ShapeDtypeStruct((rows, cut), BF16)]
    whole = [jax.ShapeDtypeStruct((rows, width), BF16)]
    pairs_of = lambda ones, twos: [ref for pair in zip(ones, twos) for ref in pair]

    across = inner(out_grad)
    beside = outer(out_grad)

    shares = []
    second = []
    for span in spans:
        (share,) = call(
            functools.partial(share_body, span), [jax.ShapeDtypeStruct((merged.shape[0], cut), BF16)], [],
            [merged, out_weight],
        )
        shares.append(share)
        (part,) = call(functools.partial(send_body, span, True), piece, [], [share, across])
        second.append(outer(part))
        merged = lax.optimization_barrier((merged, part))[0]
    beside = lax.optimization_barrier((beside, part))[0]
    across_far = [inner(beside[:, span]) for span in spans]
    g_rows = [jax.ShapeDtypeStruct((2 * rows, out_weight.shape[0]), F32)]
    (g_near,) = call(near_body, g_rows, [pltpu.VMEM((2 * rows, width), BF16)], [out_grad, beside, out_weight])
    second[0] = lax.optimization_barrier((second[0], g_near))[0]
    third = []
    to_far = []
    for at in range(HALVES):
        (sent,) = call(functools.partial(add_body, True), piece, [], [shares[at], second[at]])
        to_far.append(inner(sent))
        far = lax.optimization_barrier((across_far[at], sent))[0]
        (sent,) = call(functools.partial(send_body, slice(None), False), piece, [], [shares[at], far])
        third.append(outer(sent))
        if at + 1 < HALVES:
            states = states_of(lax.optimization_barrier((x_f, sent))[0])
            second[at + 1] = lax.optimization_barrier((second[at + 1], *states))[0]
    g_far = []
    ready = []
    for at, span in enumerate(spans):
        g_far = call(
            functools.partial(far_body, span), g_rows, [pltpu.VMEM((2 * rows, cut), BF16)],
            [second[at], third[at], across, across_far[at], out_weight, *g_far],
        )
        if at == 0:
            got = lax.optimization_barrier((to_far[0], *g_far))[0]
            ready = call(functools.partial(last_body, [slice(None)]), piece, [], [shares[0], got])
            third[-1] = lax.optimization_barrier((third[-1], *ready))[0]
    ready = call(functools.partial(last_body, spans), whole, [], [*ready, shares[-1], to_far[-1]])[0]
    (near,) = call(functools.partial(add_whole_body, spans), whole, [], pairs_of(shares, third))
    ready, near, *g_far = lax.optimization_barrier((ready, near, *g_far))

    def places():
        at = lax.axis_index("tp")
        return [at, at ^ 1, inward(False), inward(True)]

    g_f, sums = grads_of([g_near, *g_far], places, states)
    last = outer(ready)
    to_near = inner(near)
    (out,) = call(functools.partial(total_body, spans), whole, [], [*shares, last, to_near])
    return out, g_f, sums


def any_axis(out_grad, out_weight, merged, x_f, states_of, grads_of):
    parts = lax.axis_size("tp")
    gathered = lax.all_gather(out_grad, "tp", axis=0, tiled=True)
    share = jnp.dot(merged, out_weight, preferred_element_type=F32).astype(BF16)
    out = lax.psum_scatter(share, "tp", scatter_dimension=0, tiled=True)
    return out, *grads_of([back_dot(gathered, out_weight)], lambda: list(range(parts)), states_of(x_f))


def per_device(inputs, residue, log_rate, skip, out_weight, out_grad):
    blocks = lax.axis_size("ctx")
    parts = lax.axis_size("tp")
    tok, chans = inputs.shape
    seq = blocks * tok
    rows = out_grad.shape[0]
    modes = residue.shape[1]
    lanes = functools.partial(jax.ShapeDtypeStruct, dtype=F32)
    state = lanes((modes, chans))
    token_f = pltpu.VMEM((tok, chans), F32)

    (zero,) = call(clear_body, [state], [], [], flops=CLEAR_FLOPS)
    out_grad = lax.optimization_barrier((out_grad, zero))[0]
    x_f, rate, ends = call(
        functools.partial(ends_body, seq), [lanes((tok, chans)), state, lanes((2 * modes, chans))], [],
        [inputs, log_rate.T, zero],
    )
    (table,) = call(
        table_body, [lanes((3 * modes + 8, chans))], [], [rate, residue.T, skip[None, :]], flops=1_000_000_000
    )
    other_ends = from_other_core(ends, blocks)
    (pair_ends,) = call(
        functools.partial(pair_ends_body, tok, modes), [jax.ShapeDtypeStruct((2 * modes, chans), BF16)], [],
        [rate, ends, other_ends],
    )
    merged, start = call(
        functools.partial(merged_body, modes),
        [jax.ShapeDtypeStruct((tok, chans), BF16), lanes((2 * modes, chans))],
        [token_f], [x_f, table, other_ends, *from_pairs(pair_ends, blocks)],
    )

    def states_of(x_f):
        return call(
            functools.partial(states_body, modes), [lanes((tok * modes, chans))] * 2, [], [x_f, table, start]
        )

    def grads_of(pieces, places, states):
        return call(
            functools.partial(grads_body, modes, rows, places), [lanes((tok, chans)), lanes((3 * modes + 8, chans))], [],
            [x_f, table, *states, *pieces],
        )

    reduce = line_of_four if parts == 4 else any_axis
    out, g_f, sums = reduce(out_grad, out_weight, merged, x_f, states_of, grads_of)
    other_sums = from_other_core(sums, blocks)
    (pair_sums,) = call(
        functools.partial(pair_sums_body, tok, modes), [jax.ShapeDtypeStruct((4 * modes, chans), BF16)], [],
        [table, sums, other_sums],
    )
    grad_input, by_res, by_log, by_skip = call(
        functools.partial(input_body, seq, modes),
        [jax.ShapeDtypeStruct((tok, chans), BF16), state, state, lanes((1, chans))], [token_f],
        [g_f, table, other_sums, pair_sums, *from_pairs(pair_sums, blocks)],
    )
    return out, grad_input, by_res.T, by_log.T, by_skip[0]


def solution(mesh):
    placed = (
        P("ctx", "tp"),
        P("tp", None),
        P("tp", None),
        P("tp"),
        P("tp", None),
        P(("ctx", "tp"), None),
    )
    return jax.shard_map(
        per_device,
        mesh=mesh,
        in_specs=placed,
        out_specs=(P(("ctx", "tp"), None), P("ctx", "tp"), P("tp", None), P("tp", None), P("tp")),
        check_vma=False,
    )
```

```python
import functools
import math

import jax
import jax.numpy as jnp
from jax import lax
from jax.experimental import pallas as pl
from jax.experimental.pallas import tpu as pltpu
from jax.sharding import PartitionSpec as P

F32 = jnp.float32
BF16 = jnp.bfloat16
STEP = 8
CLEAR_FLOPS = 4_000_000_000
HALVES = 2


def call(body, outs, scratch, args, flops=1024):
    whole = pl.BlockSpec(memory_space=pltpu.VMEM)
    return pl.pallas_call(
        body,
        out_shape=outs,
        in_specs=[whole] * len(args),
        out_specs=[whole] * len(outs),
        scratch_shapes=scratch,
        compiler_params=pltpu.CompilerParams(vmem_limit_bytes=12 << 20),
        cost_estimate=pl.CostEstimate(flops=flops, bytes_accessed=1024, transcendentals=0),
    )(*args)


def row_of(ref, at, like):
    return jnp.broadcast_to(ref[pl.ds(at, 1), :], like.shape)


def part_of(ref, which, modes):
    return ref[pl.ds(which * modes, modes), :]


def clear_body(state_ref):
    state_ref[...] = jnp.zeros_like(state_ref)


def ends_body(seq, x_ref, log_ref, zero_ref, x_f, rate_ref, ends_ref):
    tok = x_ref.shape[0]
    modes = log_ref.shape[0]
    rate = jnp.exp(log_ref[...]) / seq
    a = jnp.exp(-rate)
    rate_ref[...] = rate
    x_f[...] = x_ref[...].astype(F32)

    def steps(block, carry):
        h, q = carry
        for inner in range(STEP):
            ah = a * h
            q = a * q + ah
            h = ah + row_of(x_f, block * STEP + inner, a)
        return h, q

    h, q = lax.fori_loop(0, tok // STEP, steps, (zero_ref[...], zero_ref[...]))
    ends_ref[pl.ds(0, modes), :] = h
    ends_ref[pl.ds(modes, modes), :] = q


def table_body(rate_ref, res_ref, skip_ref, table_ref):
    modes = rate_ref.shape[0]
    rate = rate_ref[...]
    norm = jnp.sqrt(2.0 * rate)
    table_ref[pl.ds(0, modes), :] = rate
    table_ref[pl.ds(modes, modes), :] = norm
    table_ref[pl.ds(2 * modes, modes), :] = res_ref[...] * norm
    table_ref[pl.ds(3 * modes, 8), :] = jnp.broadcast_to(skip_ref[...], (8, rate.shape[1]))


def advance(h, q, a_span, span):
    return a_span * h, a_span * (q + span * h)


def pair_ends_body(tok, modes, rate_ref, own_ref, other_ref, pair_ref):
    second = lax.axis_index("ctx") % 2 == 1
    a_chunk = jnp.exp(-(rate_ref[...] * tok))
    own = part_of(own_ref, 0, modes), part_of(own_ref, 1, modes)
    other = part_of(other_ref, 0, modes), part_of(other_ref, 1, modes)
    early = [jnp.where(second, theirs, ours) for ours, theirs in zip(own, other)]
    late = [jnp.where(second, ours, theirs) for ours, theirs in zip(own, other)]
    h, q = advance(*early, a_chunk, tok)
    pair_ref[pl.ds(0, modes), :] = (h + late[0]).astype(BF16)
    pair_ref[pl.ds(modes, modes), :] = (q + late[1]).astype(BF16)


def merged_body(modes, x_f, table_ref, other_ref, *refs):
    *far_refs, merged_ref, start_ref, y_f = refs
    tok = x_f.shape[0]
    rate = part_of(table_ref, 0, modes)
    c = part_of(table_ref, 2, modes)
    a = jnp.exp(-rate)
    a_chunk = jnp.exp(-(rate * tok))
    index = lax.axis_index("ctx")
    pair = index // 2
    h = jnp.zeros_like(a)
    q = jnp.zeros_like(a)
    for j, far in enumerate(far_refs, 1):
        apart = pair - (pair ^ j)
        since = (jnp.maximum(apart - 1, 0) * (2 * tok)).astype(F32)
        far_h, far_q = part_of(far, 0, modes).astype(F32), part_of(far, 1, modes).astype(F32)
        far_h, far_q = advance(far_h, far_q, jnp.exp(-(rate * since)), since)
        h = h + jnp.where(apart > 0, far_h, 0.0)
        q = q + jnp.where(apart > 0, far_q, 0.0)
    h_late, q_late = advance(h, q, a_chunk, tok)
    second = index % 2 == 1
    h = jnp.where(second, h_late + part_of(other_ref, 0, modes), h)
    q = jnp.where(second, q_late + part_of(other_ref, 1, modes), q)
    start_ref[pl.ds(0, modes), :] = h
    start_ref[pl.ds(modes, modes), :] = q

    def steps(block, h):
        for inner in range(STEP):
            at = block * STEP + inner
            h = a * h + row_of(x_f, at, a)
            y_f[pl.ds(at, 1), :] = jnp.sum(c * h, axis=0, keepdims=True)
        return h

    lax.fori_loop(0, tok // STEP, steps, h)
    merged_ref[...] = (y_f[...] + table_ref[pl.ds(3 * modes, 1), :] * x_f[...]).astype(BF16)


def states_body(modes, x_f, table_ref, start_ref, h_ref, q_ref):
    tok = x_f.shape[0]
    a = jnp.exp(-part_of(table_ref, 0, modes))

    def steps(block, carry):
        h, q = carry
        for inner in range(STEP):
            at = block * STEP + inner
            ah = a * h
            q = a * q + ah
            h = ah + row_of(x_f, at, a)
            to = pl.ds(pl.multiple_of(at * modes, 8), modes)
            h_ref[to, :] = h
            q_ref[to, :] = q
        return h, q

    lax.fori_loop(0, tok // STEP, steps, (part_of(start_ref, 0, modes), part_of(start_ref, 1, modes)))


def grads_body(modes, rows, places_of, x_f, table_ref, h_ref, q_ref, *refs):
    *g_refs, g_f, sums_ref = refs
    tok = x_f.shape[0]
    rate = part_of(table_ref, 0, modes)
    a = jnp.exp(-rate)
    places = places_of()
    slot = 0
    for g_ref in g_refs:
        for at in range(g_ref.shape[0] // rows):
            to = pl.multiple_of(places[slot] * rows, 8)
            g_f[pl.ds(to, rows), :] = g_ref[pl.ds(at * rows, rows), :].astype(BF16).astype(F32)
            slot += 1

    def steps(block, carry):
        power, back, by_res, by_rate = carry
        for inner in range(STEP):
            at = block * STEP + inner
            g = row_of(g_f, at, a)
            to = pl.ds(pl.multiple_of(at * modes, 8), modes)
            back = back + power * g
            power = power * a
            by_res = by_res + g * h_ref[to, :]
            by_rate = by_rate + g * q_ref[to, :]
        return power, back, by_res, by_rate

    zero = jnp.zeros_like(a)
    _, back, by_res, by_rate = lax.fori_loop(0, tok // STEP, steps, (jnp.ones_like(a), zero, zero, zero))
    sums_ref[pl.ds(0, modes), :] = back
    sums_ref[pl.ds(modes, modes), :] = by_res
    sums_ref[pl.ds(2 * modes, modes), :] = 0.5 * by_res - rate * by_rate
    direct = jnp.sum(g_f[...] * x_f[...], axis=0, keepdims=True)
    sums_ref[pl.ds(3 * modes, 8), :] = jnp.broadcast_to(direct, (8, direct.shape[1]))


def pair_sums_body(tok, modes, table_ref, own_ref, other_ref, pair_ref):
    second = lax.axis_index("ctx") % 2 == 1
    a_chunk = jnp.exp(-(part_of(table_ref, 0, modes) * tok))
    own = part_of(own_ref, 0, modes)
    other = part_of(other_ref, 0, modes)
    early = jnp.where(second, other, own)
    late = jnp.where(second, own, other)
    pair_ref[pl.ds(0, modes), :] = (early + a_chunk * late).astype(BF16)
    both = pl.ds(modes, 2 * modes)
    pair_ref[both, :] = (own_ref[both, :] + other_ref[both, :]).astype(BF16)
    direct = own_ref[pl.ds(3 * modes, 1), :] + other_ref[pl.ds(3 * modes, 1), :]
    pair_ref[pl.ds(3 * modes, modes), :] = jnp.broadcast_to(direct, own.shape).astype(BF16)


def input_body(seq, modes, g_f, table_ref, other_ref, pair_ref, *refs):
    *far_refs, grad_ref, by_res_ref, by_log_ref, by_skip_ref, y_f = refs
    tok = g_f.shape[0]
    rate = part_of(table_ref, 0, modes)
    norm = part_of(table_ref, 1, modes)
    c = part_of(table_ref, 2, modes)
    a = jnp.exp(-rate)
    a_chunk = jnp.exp(-(rate * tok))
    index = lax.axis_index("ctx")
    pair = index // 2
    z = jnp.zeros_like(a)
    for j, far in enumerate(far_refs, 1):
        apart = (pair ^ j) - pair
        until = (jnp.maximum(apart - 1, 0) * (2 * tok)).astype(F32)
        decay = jnp.exp(-(rate * until))
        z = z + jnp.where(apart > 0, decay * far[pl.ds(0, modes), :].astype(F32), 0.0)
    z = jnp.where(index % 2 == 0, a_chunk * z + part_of(other_ref, 0, modes), z)

    def steps(block, z):
        for inner in range(STEP):
            at = tok - 1 - (block * STEP + inner)
            z = a * z + row_of(g_f, at, a)
            y_f[pl.ds(at, 1), :] = jnp.sum(c * z, axis=0, keepdims=True)
        return z

    lax.fori_loop(0, tok // STEP, steps, z)
    grad_ref[...] = (y_f[...] + table_ref[pl.ds(3 * modes, 1), :] * g_f[...]).astype(BF16)
    rest = pl.ds(modes, 3 * modes)
    total = pair_ref[rest, :].astype(F32)
    for far in far_refs:
        total = total + far[rest, :].astype(F32)
    scale = 1.0 / math.sqrt(seq)
    by_res_ref[...] = scale * (norm * total[:modes])
    by_log_ref[...] = scale * (c * total[modes:2 * modes])
    by_skip_ref[...] = scale * total[2 * modes:2 * modes + 1]


def final_body(count, total, rest, *refs):
    total_refs, refs = refs[:count], refs[count:]
    out_ref = refs[-6]
    total(*total_refs, out_ref)
    rest(*refs[:-6], *refs[-5:])


def from_other_core(array, blocks):
    return lax.ppermute(array, "ctx", [(i, i ^ 1) for i in range(blocks)])


def from_pairs(array, blocks):
    return [lax.ppermute(array, "ctx", [(i, i ^ (2 * j)) for i in range(blocks)]) for j in range(1, blocks // 2)]


def outer(array):
    return lax.ppermute(array, "tp", [(0, 1), (1, 0), (2, 3), (3, 2)])


def inner(array):
    return lax.ppermute(array, "tp", [(1, 2), (2, 1), (0, 0), (3, 3)])


def back_dot(rows_in, weight):
    return lax.dot_general(rows_in, weight, (((1,), (1,)), ((), ())), preferred_element_type=F32)


def at_end():
    index = lax.axis_index("tp")
    return (index == 0) | (index == 3)


def inward(far):
    low = lax.axis_index("tp") < 2
    return jnp.where(low, 3, 0) if far else jnp.where(low, 2, 1)


def share_body(span, merged_ref, weight_ref, share_ref):
    cut = share_ref.shape[1]
    tile = min(cut, 512)
    merged = merged_ref[...]
    for at in range(0, cut, tile):
        weight = weight_ref[:, span.start + at:span.start + at + tile]
        share_ref[:, at:at + tile] = jnp.dot(merged, weight, preferred_element_type=F32).astype(BF16)


def share_rows(share_ref, at, rows):
    return share_ref[pl.ds(pl.multiple_of(at * rows, 16), rows), :]


def send_body(span, far, share_ref, passing_ref, out_ref):
    rows = out_ref.shape[0]
    end = at_end()

    @pl.when(end)
    def _():
        out_ref[...] = share_rows(share_ref, inward(far), rows)

    @pl.when(jnp.logical_not(end))
    def _():
        out_ref[...] = passing_ref[:, span]


def back_tiles(rows_ref, weight_ref, start):
    width = rows_ref.shape[1]
    tile = min(width, 1024)
    total = None
    for at in range(0, width, tile):
        part = back_dot(rows_ref[:, at:at + tile], weight_ref[:, start + at:start + at + tile])
        total = part if total is None else total + part
    return total


def near_body(own_ref, beside_ref, weight_ref, g_ref, rows_ref):
    rows = own_ref.shape[0]
    rows_ref[pl.ds(0, rows), :] = own_ref[...]
    rows_ref[pl.ds(rows, rows), :] = beside_ref[...]
    g_ref[...] = back_tiles(rows_ref, weight_ref, 0)


def far_body(span, second_ref, third_ref, across_ref, far_ref, weight_ref, *refs):
    *before_refs, g_ref, rows_ref = refs
    rows = second_ref.shape[0]
    end = at_end()

    @pl.when(end)
    def _():
        rows_ref[pl.ds(0, rows), :] = second_ref[...]
        rows_ref[pl.ds(rows, rows), :] = third_ref[...]

    @pl.when(jnp.logical_not(end))
    def _():
        rows_ref[pl.ds(0, rows), :] = across_ref[:, span]
        rows_ref[pl.ds(rows, rows), :] = far_ref[...]

    total = back_tiles(rows_ref, weight_ref, span.start)
    for before in before_refs:
        total = total + before[...]
    g_ref[...] = total


def add_body(far, share_ref, got_ref, out_ref):
    rows = out_ref.shape[0]
    block = share_rows(share_ref, inward(far), rows).astype(F32)
    out_ref[...] = (block + got_ref[...].astype(F32)).astype(BF16)


def add_whole_body(spans, *refs):
    *in_refs, out_ref = refs
    rows = out_ref.shape[0]
    for at, span in enumerate(spans):
        share_ref, got_ref = in_refs[2 * at:2 * at + 2]
        block = share_rows(share_ref, inward(False), rows).astype(F32)
        out_ref[:, span] = (block + got_ref[...].astype(F32)).astype(BF16)


def last_body(spans, *refs):
    *done_refs, share_ref, got_ref, out_ref = refs
    rows = share_ref.shape[0] // 4
    end = at_end()
    for done_ref, span in zip(done_refs, spans):
        out_ref[:, span] = done_ref[...]
    block = share_rows(share_ref, lax.axis_index("tp") ^ 1, rows).astype(F32)
    out_ref[:, spans[-1]] = (block + jnp.where(end, 0.0, got_ref[...].astype(F32))).astype(BF16)


def total_body(spans, *refs):
    *share_refs, last_ref, near_ref, out_ref = refs
    rows = out_ref.shape[0]
    end = at_end()
    for share_ref, span in zip(share_refs, spans):
        total = share_rows(share_ref, lax.axis_index("tp"), rows).astype(F32) + last_ref[:, span].astype(F32)
        out_ref[:, span] = (total + jnp.where(end, 0.0, near_ref[:, span].astype(F32))).astype(BF16)


def line_of_four(out_grad, out_weight, merged, x_f, states_of, grads_of):
    rows, width = out_grad.shape
    cut = width // HALVES
    spans = [slice(at * cut, (at + 1) * cut) for at in range(HALVES)]
    piece = [jax.ShapeDtypeStruct((rows, cut), BF16)]
    whole = [jax.ShapeDtypeStruct((rows, width), BF16)]
    pairs_of = lambda ones, twos: [ref for pair in zip(ones, twos) for ref in pair]

    across = inner(out_grad)
    beside = outer(out_grad)

    shares = []
    second = []
    for span in spans:
        (share,) = call(
            functools.partial(share_body, span), [jax.ShapeDtypeStruct((merged.shape[0], cut), BF16)], [],
            [merged, out_weight],
        )
        shares.append(share)
        (part,) = call(functools.partial(send_body, span, True), piece, [], [share, across])
        second.append(outer(part))
        merged = lax.optimization_barrier((merged, part))[0]
    beside = lax.optimization_barrier((beside, part))[0]
    across_far = [inner(beside[:, span]) for span in spans]
    g_rows = [jax.ShapeDtypeStruct((2 * rows, out_weight.shape[0]), F32)]
    (g_near,) = call(near_body, g_rows, [pltpu.VMEM((2 * rows, width), BF16)], [out_grad, beside, out_weight])
    second[0] = lax.optimization_barrier((second[0], g_near))[0]

    def far(at, before):
        return call(
            functools.partial(far_body, spans[at]), g_rows, [pltpu.VMEM((2 * rows, cut), BF16)],
            [second[at], third[at], across, across_far[at], out_weight, *before],
        )

    third = []
    to_far = []
    for at in range(HALVES):
        (sent,) = call(functools.partial(add_body, True), piece, [], [shares[at], second[at]])
        to_far.append(inner(sent))
        passing = lax.optimization_barrier((across_far[at], sent))[0]
        (sent,) = call(functools.partial(send_body, slice(None), False), piece, [], [shares[at], passing])
        third.append(outer(sent))
        if at + 1 < HALVES:
            states = states_of(lax.optimization_barrier((x_f, sent))[0])
            second[at + 1] = lax.optimization_barrier((second[at + 1], *states))[0]
    g_far = far(0, [])
    got = lax.optimization_barrier((to_far[0], *g_far))[0]
    ready = call(functools.partial(last_body, [slice(None)]), piece, [], [shares[0], got])
    (near,) = call(functools.partial(add_whole_body, spans), whole, [], pairs_of(shares, third))
    got = lax.optimization_barrier((to_far[-1], near))[0]
    (ready,) = call(functools.partial(last_body, spans), whole, [], [*ready, shares[-1], got])
    third[-1] = lax.optimization_barrier((third[-1], ready))[0]
    g_far = far(1, g_far)
    last = outer(ready)
    to_near = inner(near)

    def places():
        at = lax.axis_index("tp")
        return [at, at ^ 1, inward(False), inward(True)]

    g_f, sums = grads_of([g_near, *g_far], places, states)
    return (functools.partial(total_body, spans), whole, [*shares, last, to_near]), g_f, sums


def whole_body(total_ref, out_ref):
    out_ref[...] = total_ref[...]


def any_axis(out_grad, out_weight, merged, x_f, states_of, grads_of):
    parts = lax.axis_size("tp")
    gathered = lax.all_gather(out_grad, "tp", axis=0, tiled=True)
    share = jnp.dot(merged, out_weight, preferred_element_type=F32).astype(BF16)
    out = lax.psum_scatter(share, "tp", scatter_dimension=0, tiled=True)
    return (whole_body, [jax.ShapeDtypeStruct(out.shape, out.dtype)], [out]), *grads_of([back_dot(gathered, out_weight)], lambda: list(range(parts)), states_of(x_f))


def per_device(inputs, residue, log_rate, skip, out_weight, out_grad):
    blocks = lax.axis_size("ctx")
    parts = lax.axis_size("tp")
    tok, chans = inputs.shape
    seq = blocks * tok
    rows = out_grad.shape[0]
    modes = residue.shape[1]
    lanes = functools.partial(jax.ShapeDtypeStruct, dtype=F32)
    state = lanes((modes, chans))
    token_f = pltpu.VMEM((tok, chans), F32)

    x_f, rate, ends = call(
        functools.partial(ends_body, seq), [lanes((tok, chans)), state, lanes((2 * modes, chans))], [],
        [inputs, log_rate.T, *call(clear_body, [state], [], [], flops=CLEAR_FLOPS)], flops=2_000_000_000,
    )
    (table,) = call(
        table_body, [lanes((3 * modes + 8, chans))], [], [rate, residue.T, skip[None, :]], flops=1_000_000_000
    )
    other_ends = from_other_core(ends, blocks)
    (pair_ends,) = call(
        functools.partial(pair_ends_body, tok, modes), [jax.ShapeDtypeStruct((2 * modes, chans), BF16)], [],
        [rate, ends, other_ends],
    )
    merged, start = call(
        functools.partial(merged_body, modes),
        [jax.ShapeDtypeStruct((tok, chans), BF16), lanes((2 * modes, chans))],
        [token_f], [x_f, table, other_ends, *from_pairs(pair_ends, blocks)],
    )

    def states_of(x_f):
        return call(
            functools.partial(states_body, modes), [lanes((tok * modes, chans))] * 2, [], [x_f, table, start]
        )

    def grads_of(pieces, places, states):
        return call(
            functools.partial(grads_body, modes, rows, places), [lanes((tok, chans)), lanes((3 * modes + 8, chans))], [],
            [x_f, table, *states, *pieces],
        )

    reduce = line_of_four if parts == 4 else any_axis
    (total, out_shape, total_args), g_f, sums = reduce(out_grad, out_weight, merged, x_f, states_of, grads_of)
    other_sums = from_other_core(sums, blocks)
    (pair_sums,) = call(
        functools.partial(pair_sums_body, tok, modes), [jax.ShapeDtypeStruct((4 * modes, chans), BF16)], [],
        [table, sums, other_sums],
    )
    far_sums = from_pairs(pair_sums, blocks)
    far_sums[0] = lax.optimization_barrier((far_sums[0], total_args[-1]))[0]
    out, grad_input, by_res, by_log, by_skip = call(
        functools.partial(final_body, len(total_args), total, functools.partial(input_body, seq, modes)),
        [*out_shape, jax.ShapeDtypeStruct((tok, chans), BF16), state, state, lanes((1, chans))], [token_f],
        [*total_args, g_f, table, other_sums, pair_sums, *far_sums],
    )
    return out, grad_input, by_res.T, by_log.T, by_skip[0]


def solution(mesh):
    placed = (
        P("ctx", "tp"),
        P("tp", None),
        P("tp", None),
        P("tp"),
        P("tp", None),
        P(("ctx", "tp"), None),
    )
    return jax.shard_map(
        per_device,
        mesh=mesh,
        in_specs=placed,
        out_specs=(P(("ctx", "tp"), None), P("ctx", "tp"), P("tp", None), P("tp", None), P("tp")),
        check_vma=False,
    )
```

```python
import functools
import math

import jax
import jax.numpy as jnp
from jax import lax
from jax.experimental import pallas as pl
from jax.experimental.pallas import tpu as pltpu
from jax.sharding import PartitionSpec as P

F32 = jnp.float32
BF16 = jnp.bfloat16
STEP = 8
LOCAL_FLOPS = 1_000_000_000
CLEAR_FLOPS = 4_000_000_000
HALVES = 2


def call(body, outs, scratch, args, flops=1024, place=pltpu.VMEM):
    whole = pl.BlockSpec(memory_space=pltpu.VMEM)
    return pl.pallas_call(
        body,
        out_shape=outs,
        in_specs=[whole] * len(args),
        out_specs=[pl.BlockSpec(memory_space=place)] * len(outs),
        scratch_shapes=scratch,
        compiler_params=pltpu.CompilerParams(vmem_limit_bytes=12 << 20),
        cost_estimate=pl.CostEstimate(flops=flops, bytes_accessed=1024, transcendentals=0),
    )(*args)


def row_of(ref, at, like):
    return jnp.broadcast_to(ref[pl.ds(at, 1), :], like.shape)


def part_of(ref, which, modes):
    return ref[pl.ds(which * modes, modes), :]


def clear_body(state_ref):
    state_ref[...] = jnp.zeros_like(state_ref)


def ends_body(seq, x_ref, log_ref, zero_ref, x_f, rate_ref, ends_ref):
    tok = x_ref.shape[0]
    modes = log_ref.shape[0]
    rate = jnp.exp(log_ref[...]) / seq
    a = jnp.exp(-rate)
    rate_ref[...] = rate
    x_f[...] = x_ref[...].astype(F32)

    def steps(block, carry):
        h, q = carry
        for inner in range(STEP):
            ah = a * h
            q = a * q + ah
            h = ah + row_of(x_f, block * STEP + inner, a)
        return h, q

    h, q = lax.fori_loop(0, tok // STEP, steps, (zero_ref[...], zero_ref[...]))
    ends_ref[pl.ds(0, modes), :] = h
    ends_ref[pl.ds(modes, modes), :] = q


def table_body(rate_ref, res_ref, skip_ref, table_ref):
    modes = rate_ref.shape[0]
    rate = rate_ref[...]
    norm = jnp.sqrt(2.0 * rate)
    table_ref[pl.ds(0, modes), :] = rate
    table_ref[pl.ds(modes, modes), :] = norm
    table_ref[pl.ds(2 * modes, modes), :] = res_ref[...] * norm
    table_ref[pl.ds(3 * modes, 8), :] = jnp.broadcast_to(skip_ref[...], (8, rate.shape[1]))


def advance(h, q, a_span, span):
    return a_span * h, a_span * (q + span * h)


def pair_ends_body(tok, modes, rate_ref, own_ref, other_ref, pair_ref):
    second = lax.axis_index("ctx") % 2 == 1
    a_chunk = jnp.exp(-(rate_ref[...] * tok))
    own = part_of(own_ref, 0, modes), part_of(own_ref, 1, modes)
    other = part_of(other_ref, 0, modes), part_of(other_ref, 1, modes)
    early = [jnp.where(second, theirs, ours) for ours, theirs in zip(own, other)]
    late = [jnp.where(second, ours, theirs) for ours, theirs in zip(own, other)]
    h, q = advance(*early, a_chunk, tok)
    pair_ref[pl.ds(0, modes), :] = (h + late[0]).astype(BF16)
    pair_ref[pl.ds(modes, modes), :] = (q + late[1]).astype(BF16)


def merged_body(modes, x_f, table_ref, other_ref, *refs):
    *far_refs, merged_ref, start_ref, y_f = refs
    tok = x_f.shape[0]
    rate = part_of(table_ref, 0, modes)
    c = part_of(table_ref, 2, modes)
    a = jnp.exp(-rate)
    a_chunk = jnp.exp(-(rate * tok))
    index = lax.axis_index("ctx")
    pair = index // 2
    second = index % 2 == 1
    h = jnp.zeros_like(a)
    q = jnp.zeros_like(a)
    both = [chosen_from(far_refs, second, pl.ds(at * modes, modes)) for at in range(2)]
    for j, (far_h, far_q) in enumerate(zip(*both), 1):
        apart = pair - (pair ^ j)
        since = (jnp.maximum(apart - 1, 0) * (2 * tok)).astype(F32)
        far_h, far_q = advance(far_h, far_q, jnp.exp(-(rate * since)), since)
        h = h + jnp.where(apart > 0, far_h, 0.0)
        q = q + jnp.where(apart > 0, far_q, 0.0)
    h_late, q_late = advance(h, q, a_chunk, tok)
    h = jnp.where(second, h_late + part_of(other_ref, 0, modes), h)
    q = jnp.where(second, q_late + part_of(other_ref, 1, modes), q)
    start_ref[pl.ds(0, modes), :] = h
    start_ref[pl.ds(modes, modes), :] = q

    def steps(block, h):
        for inner in range(STEP):
            at = block * STEP + inner
            h = a * h + row_of(x_f, at, a)
            y_f[pl.ds(at, 1), :] = jnp.sum(c * h, axis=0, keepdims=True)
        return h

    lax.fori_loop(0, tok // STEP, steps, h)
    merged_ref[...] = (y_f[...] + table_ref[pl.ds(3 * modes, 1), :] * x_f[...]).astype(BF16)


def states_body(modes, x_f, table_ref, start_ref, h_ref, q_ref):
    tok = x_f.shape[0]
    a = jnp.exp(-part_of(table_ref, 0, modes))

    def steps(block, carry):
        h, q = carry
        for inner in range(STEP):
            at = block * STEP + inner
            ah = a * h
            q = a * q + ah
            h = ah + row_of(x_f, at, a)
            to = pl.ds(pl.multiple_of(at * modes, 8), modes)
            h_ref[to, :] = h
            q_ref[to, :] = q
        return h, q

    lax.fori_loop(0, tok // STEP, steps, (part_of(start_ref, 0, modes), part_of(start_ref, 1, modes)))


def grads_body(modes, rows, places_of, x_f, table_ref, h_ref, q_ref, *refs):
    *g_refs, g_f, sums_ref = refs
    tok = x_f.shape[0]
    rate = part_of(table_ref, 0, modes)
    a = jnp.exp(-rate)
    places = places_of()
    slot = 0
    for g_ref in g_refs:
        for at in range(g_ref.shape[0] // rows):
            to = pl.multiple_of(places[slot] * rows, 8)
            g_f[pl.ds(to, rows), :] = g_ref[pl.ds(at * rows, rows), :].astype(BF16).astype(F32)
            slot += 1

    def steps(block, carry):
        power, back, by_res, by_rate = carry
        for inner in range(STEP):
            at = block * STEP + inner
            g = row_of(g_f, at, a)
            to = pl.ds(pl.multiple_of(at * modes, 8), modes)
            back = back + power * g
            power = power * a
            by_res = by_res + g * h_ref[to, :]
            by_rate = by_rate + g * q_ref[to, :]
        return power, back, by_res, by_rate

    zero = jnp.zeros_like(a)
    _, back, by_res, by_rate = lax.fori_loop(0, tok // STEP, steps, (jnp.ones_like(a), zero, zero, zero))
    sums_ref[pl.ds(0, modes), :] = back
    sums_ref[pl.ds(modes, modes), :] = by_res
    sums_ref[pl.ds(2 * modes, modes), :] = 0.5 * by_res - rate * by_rate
    direct = jnp.sum(g_f[...] * x_f[...], axis=0, keepdims=True)
    sums_ref[pl.ds(3 * modes, 8), :] = jnp.broadcast_to(direct, (8, direct.shape[1]))


def pair_sums_body(tok, modes, table_ref, own_ref, other_ref, pair_ref):
    second = lax.axis_index("ctx") % 2 == 1
    a_chunk = jnp.exp(-(part_of(table_ref, 0, modes) * tok))
    own = part_of(own_ref, 0, modes)
    other = part_of(other_ref, 0, modes)
    early = jnp.where(second, other, own)
    late = jnp.where(second, own, other)
    pair_ref[pl.ds(0, modes), :] = (early + a_chunk * late).astype(BF16)
    both = pl.ds(modes, 2 * modes)
    pair_ref[both, :] = (own_ref[both, :] + other_ref[both, :]).astype(BF16)
    direct = own_ref[pl.ds(3 * modes, 1), :] + other_ref[pl.ds(3 * modes, 1), :]
    pair_ref[pl.ds(3 * modes, modes), :] = jnp.broadcast_to(direct, own.shape).astype(BF16)


def local_body(modes, g_f, table_ref, y_f):
    tok = g_f.shape[0]
    c = part_of(table_ref, 2, modes)
    a = jnp.exp(-part_of(table_ref, 0, modes))

    def steps(block, z):
        for inner in range(STEP):
            at = tok - 1 - (block * STEP + inner)
            z = a * z + row_of(g_f, at, a)
            y_f[pl.ds(at, 1), :] = jnp.sum(c * z, axis=0, keepdims=True)
        return z

    lax.fori_loop(0, tok // STEP, steps, jnp.zeros_like(a))
    y_f[...] = y_f[...] + table_ref[pl.ds(3 * modes, 1), :] * g_f[...]


def input_body(seq, modes, own_f, table_ref, other_ref, pair_ref, *refs):
    *far_refs, grad_ref, by_res_ref, by_log_ref, by_skip_ref, y_f = refs
    tok = own_f.shape[0]
    rate = part_of(table_ref, 0, modes)
    norm = part_of(table_ref, 1, modes)
    c = part_of(table_ref, 2, modes)
    a = jnp.exp(-rate)
    a_chunk = jnp.exp(-(rate * tok))
    index = lax.axis_index("ctx")
    pair = index // 2
    second = index % 2 == 1
    z = jnp.zeros_like(a)
    for j, far_z in enumerate(chosen_from(far_refs, second, pl.ds(0, modes)), 1):
        apart = (pair ^ j) - pair
        until = (jnp.maximum(apart - 1, 0) * (2 * tok)).astype(F32)
        z = z + jnp.where(apart > 0, jnp.exp(-(rate * until)) * far_z, 0.0)
    z = jnp.where(index % 2 == 0, a_chunk * z + part_of(other_ref, 0, modes), z)

    def steps(block, w):
        for inner in range(STEP):
            w = a * w
            y_f[pl.ds(tok - 1 - (block * STEP + inner), 1), :] = jnp.sum(w, axis=0, keepdims=True)
        return w

    lax.fori_loop(0, tok // STEP, steps, c * z)
    grad_ref[...] = (own_f[...] + y_f[...]).astype(BF16)
    rest = pl.ds(modes, 3 * modes)
    total = pair_ref[rest, :].astype(F32)
    for far in chosen_from(far_refs, second, rest):
        total = total + far
    scale = 1.0 / math.sqrt(seq)
    by_res_ref[...] = scale * (norm * total[:modes])
    by_log_ref[...] = scale * (c * total[modes:2 * modes])
    by_skip_ref[...] = scale * total[2 * modes:2 * modes + 1]


def from_other_core(array, blocks):
    return lax.ppermute(array, "ctx", [(i, i ^ 1) for i in range(blocks)])


def from_pairs(array, blocks):
    if blocks != 8:
        return [lax.ppermute(array, "ctx", [(i, i ^ (2 * j)) for i in range(blocks)]) for j in range(1, blocks // 2)]
    side = lax.ppermute(array, "ctx", [(i, i ^ (4 if i % 2 else 2)) for i in range(blocks)])
    corner = lax.ppermute(array, "ctx", [(i, i ^ 6) for i in range(blocks)])
    return [side, from_other_core(side, blocks), corner]


def chosen_from(refs, second, at):
    if len(refs) != 3:
        return [ref[at, :].astype(F32) for ref in refs]
    mine, swapped, corner = (ref[at, :].astype(F32) for ref in refs)
    return [jnp.where(second, swapped, mine), jnp.where(second, mine, swapped), corner]


def outer(array):
    return lax.ppermute(array, "tp", [(0, 1), (1, 0), (2, 3), (3, 2)])


def inner(array):
    return lax.ppermute(array, "tp", [(1, 2), (2, 1), (0, 0), (3, 3)])


def back_dot(rows_in, weight):
    return lax.dot_general(rows_in, weight, (((1,), (1,)), ((), ())), preferred_element_type=F32)


def at_end():
    index = lax.axis_index("tp")
    return (index == 0) | (index == 3)


def inward(far):
    low = lax.axis_index("tp") < 2
    return jnp.where(low, 3, 0) if far else jnp.where(low, 2, 1)


def share_body(span, merged_ref, weight_ref, share_ref):
    cut = share_ref.shape[1]
    tile = min(cut, 512)
    merged = merged_ref[...]
    for at in range(0, cut, tile):
        weight = weight_ref[:, span.start + at:span.start + at + tile]
        share_ref[:, at:at + tile] = jnp.dot(merged, weight, preferred_element_type=F32).astype(BF16)


def share_rows(share_ref, at, rows):
    return share_ref[pl.ds(pl.multiple_of(at * rows, 16), rows), :]


def send_body(span, far, share_ref, passing_ref, out_ref):
    rows = out_ref.shape[0]
    end = at_end()

    @pl.when(end)
    def _():
        out_ref[...] = share_rows(share_ref, inward(far), rows)

    @pl.when(jnp.logical_not(end))
    def _():
        out_ref[...] = passing_ref[:, span]


def back_tiles(rows_ref, weight_ref, start):
    width = rows_ref.shape[1]
    tile = min(width, 1024)
    total = None
    for at in range(0, width, tile):
        part = back_dot(rows_ref[:, at:at + tile], weight_ref[:, start + at:start + at + tile])
        total = part if total is None else total + part
    return total


def near_body(own_ref, beside_ref, weight_ref, g_ref, rows_ref):
    rows = own_ref.shape[0]
    rows_ref[pl.ds(0, rows), :] = own_ref[...]
    rows_ref[pl.ds(rows, rows), :] = beside_ref[...]
    g_ref[...] = back_tiles(rows_ref, weight_ref, 0)


def far_body(span, second_ref, third_ref, across_ref, far_ref, weight_ref, *refs):
    *before_refs, g_ref, rows_ref = refs
    rows = second_ref.shape[0]
    end = at_end()

    @pl.when(end)
    def _():
        rows_ref[pl.ds(0, rows), :] = second_ref[...]
        rows_ref[pl.ds(rows, rows), :] = third_ref[...]

    @pl.when(jnp.logical_not(end))
    def _():
        rows_ref[pl.ds(0, rows), :] = across_ref[:, span]
        rows_ref[pl.ds(rows, rows), :] = far_ref[...]

    total = back_tiles(rows_ref, weight_ref, span.start)
    for before in before_refs:
        total = total + before[...]
    g_ref[...] = total


def add_body(far, share_ref, got_ref, out_ref):
    rows = out_ref.shape[0]
    block = share_rows(share_ref, inward(far), rows).astype(F32)
    out_ref[...] = (block + got_ref[...].astype(F32)).astype(BF16)


def add_whole_body(spans, *refs):
    *in_refs, out_ref = refs
    rows = out_ref.shape[0]
    for at, span in enumerate(spans):
        share_ref, got_ref = in_refs[2 * at:2 * at + 2]
        block = share_rows(share_ref, inward(False), rows).astype(F32)
        out_ref[:, span] = (block + got_ref[...].astype(F32)).astype(BF16)


def last_body(spans, *refs):
    *done_refs, share_ref, got_ref, out_ref = refs
    rows = share_ref.shape[0] // 4
    end = at_end()
    for done_ref, span in zip(done_refs, spans):
        out_ref[:, span] = done_ref[...]
    block = share_rows(share_ref, lax.axis_index("tp") ^ 1, rows).astype(F32)
    out_ref[:, spans[-1]] = (block + jnp.where(end, 0.0, got_ref[...].astype(F32))).astype(BF16)


def total_body(spans, *refs):
    *share_refs, last_ref, near_ref, out_far, out_ref, sems = refs
    rows = out_ref.shape[0]
    end = at_end()
    copies = []
    for at, (share_ref, span) in enumerate(zip(share_refs, spans)):
        total = share_rows(share_ref, lax.axis_index("tp"), rows).astype(F32) + last_ref[:, span].astype(F32)
        out_ref[:, span] = (total + jnp.where(end, 0.0, near_ref[:, span].astype(F32))).astype(BF16)
        copies.append(pltpu.make_async_copy(out_ref.at[:, span], out_far.at[:, span], sems.at[at]))
        copies[-1].start()
    for copy in copies:
        copy.wait()


def line_of_four(out_grad, out_weight, merged, x_f, states_of, grads_of):
    rows, width = out_grad.shape
    cut = width // HALVES
    spans = [slice(at * cut, (at + 1) * cut) for at in range(HALVES)]
    piece = [jax.ShapeDtypeStruct((rows, cut), BF16)]
    whole = [jax.ShapeDtypeStruct((rows, width), BF16)]
    pairs_of = lambda ones, twos: [ref for pair in zip(ones, twos) for ref in pair]

    across = inner(out_grad)
    beside = outer(out_grad)

    shares = []
    second = []
    for span in spans:
        (share,) = call(
            functools.partial(share_body, span), [jax.ShapeDtypeStruct((merged.shape[0], cut), BF16)], [],
            [merged, out_weight],
        )
        shares.append(share)
        (part,) = call(functools.partial(send_body, span, True), piece, [], [share, across])
        second.append(outer(part))
        merged = lax.optimization_barrier((merged, part))[0]
    beside = lax.optimization_barrier((beside, part))[0]
    across_far = [inner(beside[:, span]) for span in spans]
    g_rows = [jax.ShapeDtypeStruct((2 * rows, out_weight.shape[0]), F32)]
    (g_near,) = call(near_body, g_rows, [pltpu.VMEM((2 * rows, width), BF16)], [out_grad, beside, out_weight])
    second[0] = lax.optimization_barrier((second[0], g_near))[0]
    third = []
    to_far = []
    for at in range(HALVES):
        (sent,) = call(functools.partial(add_body, True), piece, [], [shares[at], second[at]])
        to_far.append(inner(sent))
        far = lax.optimization_barrier((across_far[at], sent))[0]
        (sent,) = call(functools.partial(send_body, slice(None), False), piece, [], [shares[at], far])
        third.append(outer(sent))
        if at + 1 < HALVES:
            states = states_of(lax.optimization_barrier((x_f, sent))[0])
            second[at + 1] = lax.optimization_barrier((second[at + 1], *states))[0]
    g_far = []
    ready = []
    for at, span in enumerate(spans):
        g_far = call(
            functools.partial(far_body, span), g_rows, [pltpu.VMEM((2 * rows, cut), BF16)],
            [second[at], third[at], across, across_far[at], out_weight, *g_far],
        )
        if at == 0:
            got = lax.optimization_barrier((to_far[0], *g_far))[0]
            ready = call(functools.partial(last_body, [slice(None)]), piece, [], [shares[0], got])
            third[-1] = lax.optimization_barrier((third[-1], *ready))[0]
    ready = call(functools.partial(last_body, spans), whole, [], [*ready, shares[-1], to_far[-1]])[0]
    (near,) = call(functools.partial(add_whole_body, spans), whole, [], pairs_of(shares, third))
    ready, near, *g_far = lax.optimization_barrier((ready, near, *g_far))

    def places():
        at = lax.axis_index("tp")
        return [at, at ^ 1, inward(False), inward(True)]

    g_f, sums = grads_of([g_near, *g_far], places, states)
    last = outer(ready)
    to_near = inner(near)
    (out,) = call(
        functools.partial(total_body, spans), whole,
        [pltpu.VMEM((rows, width), BF16), pltpu.SemaphoreType.DMA((len(spans),))],
        [*shares, last, to_near], place=pl.ANY,
    )
    return out, g_f, sums


def any_axis(out_grad, out_weight, merged, x_f, states_of, grads_of):
    parts = lax.axis_size("tp")
    gathered = lax.all_gather(out_grad, "tp", axis=0, tiled=True)
    share = jnp.dot(merged, out_weight, preferred_element_type=F32).astype(BF16)
    out = lax.psum_scatter(share, "tp", scatter_dimension=0, tiled=True)
    return out, *grads_of([back_dot(gathered, out_weight)], lambda: list(range(parts)), states_of(x_f))


def per_device(inputs, residue, log_rate, skip, out_weight, out_grad):
    blocks = lax.axis_size("ctx")
    parts = lax.axis_size("tp")
    tok, chans = inputs.shape
    seq = blocks * tok
    rows = out_grad.shape[0]
    modes = residue.shape[1]
    lanes = functools.partial(jax.ShapeDtypeStruct, dtype=F32)
    state = lanes((modes, chans))
    token_f = pltpu.VMEM((tok, chans), F32)

    x_f, rate, ends = call(
        functools.partial(ends_body, seq), [lanes((tok, chans)), state, lanes((2 * modes, chans))], [],
        [inputs, log_rate.T, *call(clear_body, [state], [], [], flops=CLEAR_FLOPS)], flops=2_000_000_000,
    )
    (table,) = call(
        table_body, [lanes((3 * modes + 8, chans))], [], [rate, residue.T, skip[None, :]], flops=1_000_000_000
    )
    other_ends = from_other_core(ends, blocks)
    (pair_ends,) = call(
        functools.partial(pair_ends_body, tok, modes), [jax.ShapeDtypeStruct((2 * modes, chans), BF16)], [],
        [rate, ends, other_ends],
    )
    merged, start = call(
        functools.partial(merged_body, modes),
        [jax.ShapeDtypeStruct((tok, chans), BF16), lanes((2 * modes, chans))],
        [token_f], [x_f, table, other_ends, *from_pairs(pair_ends, blocks)],
    )

    def states_of(x_f):
        return call(
            functools.partial(states_body, modes), [lanes((tok * modes, chans))] * 2, [], [x_f, table, start]
        )

    def grads_of(pieces, places, states):
        return call(
            functools.partial(grads_body, modes, rows, places), [lanes((tok, chans)), lanes((3 * modes + 8, chans))], [],
            [x_f, table, *states, *pieces],
        )

    reduce = line_of_four if parts == 4 else any_axis
    out, g_f, sums = reduce(out_grad, out_weight, merged, x_f, states_of, grads_of)
    (own_grad,) = call(functools.partial(local_body, modes), [lanes((tok, chans))], [], [g_f, table], flops=LOCAL_FLOPS)
    other_sums = from_other_core(sums, blocks)
    (pair_sums,) = call(
        functools.partial(pair_sums_body, tok, modes), [jax.ShapeDtypeStruct((4 * modes, chans), BF16)], [],
        [table, sums, other_sums],
    )
    grad_input, by_res, by_log, by_skip = call(
        functools.partial(input_body, seq, modes),
        [jax.ShapeDtypeStruct((tok, chans), BF16), state, state, lanes((1, chans))], [token_f],
        [own_grad, table, other_sums, pair_sums, *from_pairs(pair_sums, blocks)],
    )
    return out, grad_input, by_res.T, by_log.T, by_skip[0]


def solution(mesh):
    placed = (
        P("ctx", "tp"),
        P("tp", None),
        P("tp", None),
        P("tp"),
        P("tp", None),
        P(("ctx", "tp"), None),
    )
    return jax.shard_map(
        per_device,
        mesh=mesh,
        in_specs=placed,
        out_specs=(P(("ctx", "tp"), None), P("ctx", "tp"), P("tp", None), P("tp", None), P("tp")),
        check_vma=False,
    )
```

```python
import functools
import math

import jax
import jax.numpy as jnp
from jax import lax
from jax.experimental import pallas as pl
from jax.experimental.pallas import tpu as pltpu
from jax.sharding import PartitionSpec as P

F32 = jnp.float32
BF16 = jnp.bfloat16
STEP = 8
LOCAL_FLOPS = 1_000_000_000
CLEAR_FLOPS = 4_000_000_000
HALVES = 2


def call(body, outs, scratch, args, flops=1024, place=pltpu.VMEM):
    whole = pl.BlockSpec(memory_space=pltpu.VMEM)
    return pl.pallas_call(
        body,
        out_shape=outs,
        in_specs=[whole] * len(args),
        out_specs=[pl.BlockSpec(memory_space=place)] * len(outs),
        scratch_shapes=scratch,
        compiler_params=pltpu.CompilerParams(vmem_limit_bytes=12 << 20),
        cost_estimate=pl.CostEstimate(flops=flops, bytes_accessed=1024, transcendentals=0),
    )(*args)


def row_of(ref, at, like):
    return jnp.broadcast_to(ref[pl.ds(at, 1), :], like.shape)


def part_of(ref, which, modes):
    return ref[pl.ds(which * modes, modes), :]


def clear_body(state_ref):
    state_ref[...] = jnp.zeros_like(state_ref)


def ends_body(seq, x_ref, log_ref, zero_ref, x_f, rate_ref, ends_ref):
    tok = x_ref.shape[0]
    modes = log_ref.shape[0]
    rate = jnp.exp(log_ref[...]) / seq
    a = jnp.exp(-rate)
    rate_ref[...] = rate
    x_f[...] = x_ref[...].astype(F32)

    def steps(block, carry):
        h, q = carry
        for inner in range(STEP):
            ah = a * h
            q = a * q + ah
            h = ah + row_of(x_f, block * STEP + inner, a)
        return h, q

    h, q = lax.fori_loop(0, tok // STEP, steps, (zero_ref[...], zero_ref[...]))
    ends_ref[pl.ds(0, modes), :] = h
    ends_ref[pl.ds(modes, modes), :] = q


def table_body(rate_ref, res_ref, skip_ref, table_ref):
    modes = rate_ref.shape[0]
    rate = rate_ref[...]
    norm = jnp.sqrt(2.0 * rate)
    table_ref[pl.ds(0, modes), :] = rate
    table_ref[pl.ds(modes, modes), :] = norm
    table_ref[pl.ds(2 * modes, modes), :] = res_ref[...] * norm
    table_ref[pl.ds(3 * modes, 8), :] = jnp.broadcast_to(skip_ref[...], (8, rate.shape[1]))


def advance(h, q, a_span, span):
    return a_span * h, a_span * (q + span * h)


def pair_ends_body(tok, modes, rate_ref, own_ref, other_ref, pair_ref):
    second = lax.axis_index("ctx") % 2 == 1
    a_chunk = jnp.exp(-(rate_ref[...] * tok))
    own = part_of(own_ref, 0, modes), part_of(own_ref, 1, modes)
    other = part_of(other_ref, 0, modes), part_of(other_ref, 1, modes)
    early = [jnp.where(second, theirs, ours) for ours, theirs in zip(own, other)]
    late = [jnp.where(second, ours, theirs) for ours, theirs in zip(own, other)]
    h, q = advance(*early, a_chunk, tok)
    pair_ref[pl.ds(0, modes), :] = (h + late[0]).astype(BF16)
    pair_ref[pl.ds(modes, modes), :] = (q + late[1]).astype(BF16)


def merged_body(modes, x_f, table_ref, other_ref, *refs):
    *far_refs, merged_ref, start_ref, y_f = refs
    tok = x_f.shape[0]
    rate = part_of(table_ref, 0, modes)
    c = part_of(table_ref, 2, modes)
    a = jnp.exp(-rate)
    a_chunk = jnp.exp(-(rate * tok))
    index = lax.axis_index("ctx")
    pair = index // 2
    second = index % 2 == 1
    h = jnp.zeros_like(a)
    q = jnp.zeros_like(a)
    both = [chosen_from(far_refs, second, pl.ds(at * modes, modes)) for at in range(2)]
    for j, (far_h, far_q) in enumerate(zip(*both), 1):
        apart = pair - (pair ^ j)
        since = (jnp.maximum(apart - 1, 0) * (2 * tok)).astype(F32)
        far_h, far_q = advance(far_h, far_q, jnp.exp(-(rate * since)), since)
        h = h + jnp.where(apart > 0, far_h, 0.0)
        q = q + jnp.where(apart > 0, far_q, 0.0)
    h_late, q_late = advance(h, q, a_chunk, tok)
    h = jnp.where(second, h_late + part_of(other_ref, 0, modes), h)
    q = jnp.where(second, q_late + part_of(other_ref, 1, modes), q)
    start_ref[pl.ds(0, modes), :] = h
    start_ref[pl.ds(modes, modes), :] = q

    def steps(block, h):
        for inner in range(STEP):
            at = block * STEP + inner
            h = a * h + row_of(x_f, at, a)
            y_f[pl.ds(at, 1), :] = jnp.sum(c * h, axis=0, keepdims=True)
        return h

    lax.fori_loop(0, tok // STEP, steps, h)
    merged_ref[...] = (y_f[...] + table_ref[pl.ds(3 * modes, 1), :] * x_f[...]).astype(BF16)


def states_body(modes, x_f, table_ref, start_ref, h_ref, q_ref):
    tok = x_f.shape[0]
    a = jnp.exp(-part_of(table_ref, 0, modes))

    def steps(block, carry):
        h, q = carry
        for inner in range(STEP):
            at = block * STEP + inner
            ah = a * h
            q = a * q + ah
            h = ah + row_of(x_f, at, a)
            to = pl.ds(pl.multiple_of(at * modes, 8), modes)
            h_ref[to, :] = h
            q_ref[to, :] = q
        return h, q

    lax.fori_loop(0, tok // STEP, steps, (part_of(start_ref, 0, modes), part_of(start_ref, 1, modes)))


def grads_body(modes, rows, places_of, x_f, table_ref, h_ref, q_ref, *refs):
    *g_refs, g_f, sums_ref = refs
    tok = x_f.shape[0]
    rate = part_of(table_ref, 0, modes)
    a = jnp.exp(-rate)
    places = places_of()
    slot = 0
    for g_ref in g_refs:
        for at in range(g_ref.shape[0] // rows):
            to = pl.multiple_of(places[slot] * rows, 8)
            g_f[pl.ds(to, rows), :] = g_ref[pl.ds(at * rows, rows), :].astype(BF16).astype(F32)
            slot += 1

    def steps(block, carry):
        power, back, by_res, by_rate = carry
        for inner in range(STEP):
            at = block * STEP + inner
            g = row_of(g_f, at, a)
            to = pl.ds(pl.multiple_of(at * modes, 8), modes)
            back = back + power * g
            power = power * a
            by_res = by_res + g * h_ref[to, :]
            by_rate = by_rate + g * q_ref[to, :]
        return power, back, by_res, by_rate

    zero = jnp.zeros_like(a)
    _, back, by_res, by_rate = lax.fori_loop(0, tok // STEP, steps, (jnp.ones_like(a), zero, zero, zero))
    sums_ref[pl.ds(0, modes), :] = back
    sums_ref[pl.ds(modes, modes), :] = by_res
    sums_ref[pl.ds(2 * modes, modes), :] = 0.5 * by_res - rate * by_rate
    direct = jnp.sum(g_f[...] * x_f[...], axis=0, keepdims=True)
    sums_ref[pl.ds(3 * modes, 8), :] = jnp.broadcast_to(direct, (8, direct.shape[1]))


def pair_sums_body(tok, modes, table_ref, own_ref, other_ref, pair_ref):
    second = lax.axis_index("ctx") % 2 == 1
    a_chunk = jnp.exp(-(part_of(table_ref, 0, modes) * tok))
    own = part_of(own_ref, 0, modes)
    other = part_of(other_ref, 0, modes)
    early = jnp.where(second, other, own)
    late = jnp.where(second, own, other)
    pair_ref[pl.ds(0, modes), :] = (early + a_chunk * late).astype(BF16)
    both = pl.ds(modes, 2 * modes)
    pair_ref[both, :] = (own_ref[both, :] + other_ref[both, :]).astype(BF16)
    direct = own_ref[pl.ds(3 * modes, 1), :] + other_ref[pl.ds(3 * modes, 1), :]
    pair_ref[pl.ds(3 * modes, modes), :] = jnp.broadcast_to(direct, own.shape).astype(BF16)


def local_body(modes, g_f, table_ref, y_f, powers_ref):
    tok = g_f.shape[0]
    ahead = 8 - lax.broadcasted_iota(jnp.int32, (8, g_f.shape[1]), 0)
    for mode in range(modes):
        rate = jnp.broadcast_to(table_ref[pl.ds(mode, 1), :], ahead.shape)
        powers_ref[pl.ds(8 * mode, 8), :] = jnp.exp(-(rate * ahead.astype(F32)))
    c = part_of(table_ref, 2, modes)
    a = jnp.exp(-part_of(table_ref, 0, modes))

    def steps(block, z):
        for inner in range(STEP):
            at = tok - 1 - (block * STEP + inner)
            z = a * z + row_of(g_f, at, a)
            y_f[pl.ds(at, 1), :] = jnp.sum(c * z, axis=0, keepdims=True)
        return z

    lax.fori_loop(0, tok // STEP, steps, jnp.zeros_like(a))
    y_f[...] = y_f[...] + table_ref[pl.ds(3 * modes, 1), :] * g_f[...]


def input_body(seq, modes, own_f, powers_ref, table_ref, other_ref, pair_ref, *refs):
    *far_refs, grad_ref, by_res_ref, by_log_ref, by_skip_ref, y_f, w_ref = refs
    tok = own_f.shape[0]
    rate = part_of(table_ref, 0, modes)
    norm = part_of(table_ref, 1, modes)
    c = part_of(table_ref, 2, modes)
    a_chunk = jnp.exp(-(rate * tok))
    a_block = jnp.exp(-(rate * 8.0))
    index = lax.axis_index("ctx")
    pair = index // 2
    second = index % 2 == 1
    z = jnp.zeros_like(rate)
    for j, far_z in enumerate(chosen_from(far_refs, second, pl.ds(0, modes)), 1):
        apart = (pair ^ j) - pair
        until = (jnp.maximum(apart - 1, 0) * (2 * tok)).astype(F32)
        z = z + jnp.where(apart > 0, jnp.exp(-(rate * until)) * far_z, 0.0)
    z = jnp.where(index % 2 == 0, a_chunk * z + part_of(other_ref, 0, modes), z)

    w_ref[...] = c * z

    def steps(block, carry):
        total = None
        for mode in range(modes):
            part = row_of(w_ref, mode, powers_ref[pl.ds(0, 8), :]) * powers_ref[pl.ds(8 * mode, 8), :]
            total = part if total is None else total + part
        y_f[pl.ds(pl.multiple_of(tok - 8 * (block + 1), 8), 8), :] = total
        w_ref[...] = a_block * w_ref[...]
        return carry

    lax.fori_loop(0, tok // 8, steps, 0)
    grad_ref[...] = (own_f[...] + y_f[...]).astype(BF16)
    rest = pl.ds(modes, 3 * modes)
    total = pair_ref[rest, :].astype(F32)
    for far in chosen_from(far_refs, second, rest):
        total = total + far
    scale = 1.0 / math.sqrt(seq)
    by_res_ref[...] = scale * (norm * total[:modes])
    by_log_ref[...] = scale * (c * total[modes:2 * modes])
    by_skip_ref[...] = scale * total[2 * modes:2 * modes + 1]


def from_other_core(array, blocks):
    return lax.ppermute(array, "ctx", [(i, i ^ 1) for i in range(blocks)])


def from_pairs(array, blocks):
    if blocks != 8:
        return [lax.ppermute(array, "ctx", [(i, i ^ (2 * j)) for i in range(blocks)]) for j in range(1, blocks // 2)]
    side = lax.ppermute(array, "ctx", [(i, i ^ (4 if i % 2 else 2)) for i in range(blocks)])
    corner = lax.ppermute(array, "ctx", [(i, i ^ 6) for i in range(blocks)])
    return [side, from_other_core(side, blocks), corner]


def chosen_from(refs, second, at):
    if len(refs) != 3:
        return [ref[at, :].astype(F32) for ref in refs]
    mine, swapped, corner = (ref[at, :].astype(F32) for ref in refs)
    return [jnp.where(second, swapped, mine), jnp.where(second, mine, swapped), corner]


def outer(array):
    return lax.ppermute(array, "tp", [(0, 1), (1, 0), (2, 3), (3, 2)])


def inner(array):
    return lax.ppermute(array, "tp", [(1, 2), (2, 1), (0, 0), (3, 3)])


def back_dot(rows_in, weight):
    return lax.dot_general(rows_in, weight, (((1,), (1,)), ((), ())), preferred_element_type=F32)


def at_end():
    index = lax.axis_index("tp")
    return (index == 0) | (index == 3)


def inward(far):
    low = lax.axis_index("tp") < 2
    return jnp.where(low, 3, 0) if far else jnp.where(low, 2, 1)


def share_body(span, merged_ref, weight_ref, share_ref):
    cut = share_ref.shape[1]
    tile = min(cut, 512)
    merged = merged_ref[...]
    for at in range(0, cut, tile):
        weight = weight_ref[:, span.start + at:span.start + at + tile]
        share_ref[:, at:at + tile] = jnp.dot(merged, weight, preferred_element_type=F32).astype(BF16)


def share_rows(share_ref, at, rows):
    return share_ref[pl.ds(pl.multiple_of(at * rows, 16), rows), :]


def send_body(span, far, share_ref, passing_ref, out_ref):
    rows = out_ref.shape[0]
    end = at_end()

    @pl.when(end)
    def _():
        out_ref[...] = share_rows(share_ref, inward(far), rows)

    @pl.when(jnp.logical_not(end))
    def _():
        out_ref[...] = passing_ref[:, span]


def back_tiles(rows_ref, weight_ref, start):
    width = rows_ref.shape[1]
    tile = min(width, 1024)
    total = None
    for at in range(0, width, tile):
        part = back_dot(rows_ref[:, at:at + tile], weight_ref[:, start + at:start + at + tile])
        total = part if total is None else total + part
    return total


def near_body(own_ref, beside_ref, weight_ref, g_ref, rows_ref):
    rows = own_ref.shape[0]
    rows_ref[pl.ds(0, rows), :] = own_ref[...]
    rows_ref[pl.ds(rows, rows), :] = beside_ref[...]
    g_ref[...] = back_tiles(rows_ref, weight_ref, 0)


def far_body(span, second_ref, third_ref, across_ref, far_ref, weight_ref, *refs):
    *before_refs, g_ref, rows_ref = refs
    rows = second_ref.shape[0]
    end = at_end()

    @pl.when(end)
    def _():
        rows_ref[pl.ds(0, rows), :] = second_ref[...]
        rows_ref[pl.ds(rows, rows), :] = third_ref[...]

    @pl.when(jnp.logical_not(end))
    def _():
        rows_ref[pl.ds(0, rows), :] = across_ref[:, span]
        rows_ref[pl.ds(rows, rows), :] = far_ref[...]

    total = back_tiles(rows_ref, weight_ref, span.start)
    for before in before_refs:
        total = total + before[...]
    g_ref[...] = total


def add_body(far, share_ref, got_ref, out_ref):
    rows = out_ref.shape[0]
    block = share_rows(share_ref, inward(far), rows).astype(F32)
    out_ref[...] = (block + got_ref[...].astype(F32)).astype(BF16)


def add_whole_body(spans, *refs):
    *in_refs, out_ref = refs
    rows = out_ref.shape[0]
    for at, span in enumerate(spans):
        share_ref, got_ref = in_refs[2 * at:2 * at + 2]
        block = share_rows(share_ref, inward(False), rows).astype(F32)
        out_ref[:, span] = (block + got_ref[...].astype(F32)).astype(BF16)


def last_body(spans, *refs):
    *done_refs, share_ref, got_ref, out_ref = refs
    rows = share_ref.shape[0] // 4
    end = at_end()
    for done_ref, span in zip(done_refs, spans):
        out_ref[:, span] = done_ref[...]
    block = share_rows(share_ref, lax.axis_index("tp") ^ 1, rows).astype(F32)
    out_ref[:, spans[-1]] = (block + jnp.where(end, 0.0, got_ref[...].astype(F32))).astype(BF16)


def total_body(spans, *refs):
    *share_refs, last_ref, near_ref, out_far, out_ref, sems = refs
    rows = out_ref.shape[0]
    end = at_end()
    copies = []
    for at, (share_ref, span) in enumerate(zip(share_refs, spans)):
        total = share_rows(share_ref, lax.axis_index("tp"), rows).astype(F32) + last_ref[:, span].astype(F32)
        out_ref[:, span] = (total + jnp.where(end, 0.0, near_ref[:, span].astype(F32))).astype(BF16)
        copies.append(pltpu.make_async_copy(out_ref.at[:, span], out_far.at[:, span], sems.at[at]))
        copies[-1].start()
    for copy in copies:
        copy.wait()


def line_of_four(out_grad, out_weight, merged, x_f, states_of, grads_of):
    rows, width = out_grad.shape
    cut = width // HALVES
    spans = [slice(at * cut, (at + 1) * cut) for at in range(HALVES)]
    piece = [jax.ShapeDtypeStruct((rows, cut), BF16)]
    whole = [jax.ShapeDtypeStruct((rows, width), BF16)]
    pairs_of = lambda ones, twos: [ref for pair in zip(ones, twos) for ref in pair]

    across = inner(out_grad)
    beside = outer(out_grad)

    shares = []
    second = []
    for span in spans:
        (share,) = call(
            functools.partial(share_body, span), [jax.ShapeDtypeStruct((merged.shape[0], cut), BF16)], [],
            [merged, out_weight],
        )
        shares.append(share)
        (part,) = call(functools.partial(send_body, span, True), piece, [], [share, across])
        second.append(outer(part))
        merged = lax.optimization_barrier((merged, part))[0]
    beside = lax.optimization_barrier((beside, part))[0]
    across_far = [inner(beside[:, span]) for span in spans]
    g_rows = [jax.ShapeDtypeStruct((2 * rows, out_weight.shape[0]), F32)]
    (g_near,) = call(near_body, g_rows, [pltpu.VMEM((2 * rows, width), BF16)], [out_grad, beside, out_weight])
    second[0] = lax.optimization_barrier((second[0], g_near))[0]
    third = []
    to_far = []
    for at in range(HALVES):
        (sent,) = call(functools.partial(add_body, True), piece, [], [shares[at], second[at]])
        to_far.append(inner(sent))
        far = lax.optimization_barrier((across_far[at], sent))[0]
        (sent,) = call(functools.partial(send_body, slice(None), False), piece, [], [shares[at], far])
        third.append(outer(sent))
        if at + 1 < HALVES:
            states = states_of(lax.optimization_barrier((x_f, sent))[0])
            second[at + 1] = lax.optimization_barrier((second[at + 1], *states))[0]
    g_far = []
    ready = []
    for at, span in enumerate(spans):
        g_far = call(
            functools.partial(far_body, span), g_rows, [pltpu.VMEM((2 * rows, cut), BF16)],
            [second[at], third[at], across, across_far[at], out_weight, *g_far],
        )
        if at == 0:
            got = lax.optimization_barrier((to_far[0], *g_far))[0]
            ready = call(functools.partial(last_body, [slice(None)]), piece, [], [shares[0], got])
            third[-1] = lax.optimization_barrier((third[-1], *ready))[0]
    ready = call(functools.partial(last_body, spans), whole, [], [*ready, shares[-1], to_far[-1]])[0]
    (near,) = call(functools.partial(add_whole_body, spans), whole, [], pairs_of(shares, third))
    ready, near, *g_far = lax.optimization_barrier((ready, near, *g_far))

    def places():
        at = lax.axis_index("tp")
        return [at, at ^ 1, inward(False), inward(True)]

    g_f, sums = grads_of([g_near, *g_far], places, states)
    last = outer(ready)
    to_near = inner(near)
    (out,) = call(
        functools.partial(total_body, spans), whole,
        [pltpu.VMEM((rows, width), BF16), pltpu.SemaphoreType.DMA((len(spans),))],
        [*shares, last, to_near], place=pl.ANY,
    )
    return out, g_f, sums


def any_axis(out_grad, out_weight, merged, x_f, states_of, grads_of):
    parts = lax.axis_size("tp")
    gathered = lax.all_gather(out_grad, "tp", axis=0, tiled=True)
    share = jnp.dot(merged, out_weight, preferred_element_type=F32).astype(BF16)
    out = lax.psum_scatter(share, "tp", scatter_dimension=0, tiled=True)
    return out, *grads_of([back_dot(gathered, out_weight)], lambda: list(range(parts)), states_of(x_f))


def per_device(inputs, residue, log_rate, skip, out_weight, out_grad):
    blocks = lax.axis_size("ctx")
    parts = lax.axis_size("tp")
    tok, chans = inputs.shape
    seq = blocks * tok
    rows = out_grad.shape[0]
    modes = residue.shape[1]
    lanes = functools.partial(jax.ShapeDtypeStruct, dtype=F32)
    state = lanes((modes, chans))
    token_f = pltpu.VMEM((tok, chans), F32)

    x_f, rate, ends = call(
        functools.partial(ends_body, seq), [lanes((tok, chans)), state, lanes((2 * modes, chans))], [],
        [inputs, log_rate.T, *call(clear_body, [state], [], [], flops=CLEAR_FLOPS)], flops=2_000_000_000,
    )
    (table,) = call(
        table_body, [lanes((3 * modes + 8, chans))], [], [rate, residue.T, skip[None, :]], flops=1_000_000_000
    )
    other_ends = from_other_core(ends, blocks)
    (pair_ends,) = call(
        functools.partial(pair_ends_body, tok, modes), [jax.ShapeDtypeStruct((2 * modes, chans), BF16)], [],
        [rate, ends, other_ends],
    )
    merged, start = call(
        functools.partial(merged_body, modes),
        [jax.ShapeDtypeStruct((tok, chans), BF16), lanes((2 * modes, chans))],
        [token_f], [x_f, table, other_ends, *from_pairs(pair_ends, blocks)],
    )

    def states_of(x_f):
        return call(
            functools.partial(states_body, modes), [lanes((tok * modes, chans))] * 2, [], [x_f, table, start]
        )

    def grads_of(pieces, places, states):
        return call(
            functools.partial(grads_body, modes, rows, places), [lanes((tok, chans)), lanes((3 * modes + 8, chans))], [],
            [x_f, table, *states, *pieces],
        )

    reduce = line_of_four if parts == 4 else any_axis
    out, g_f, sums = reduce(out_grad, out_weight, merged, x_f, states_of, grads_of)
    own_grad, powers = call(
        functools.partial(local_body, modes), [lanes((tok, chans)), lanes((8 * modes, chans))], [], [g_f, table],
        flops=LOCAL_FLOPS,
    )
    other_sums = from_other_core(sums, blocks)
    (pair_sums,) = call(
        functools.partial(pair_sums_body, tok, modes), [jax.ShapeDtypeStruct((4 * modes, chans), BF16)], [],
        [table, sums, other_sums],
    )
    grad_input, by_res, by_log, by_skip = call(
        functools.partial(input_body, seq, modes),
        [jax.ShapeDtypeStruct((tok, chans), BF16), state, state, lanes((1, chans))], [token_f, pltpu.VMEM((modes, chans), F32)],
        [own_grad, powers, table, other_sums, pair_sums, *from_pairs(pair_sums, blocks)],
    )
    return out, grad_input, by_res.T, by_log.T, by_skip[0]


def solution(mesh):
    placed = (
        P("ctx", "tp"),
        P("tp", None),
        P("tp", None),
        P("tp"),
        P("tp", None),
        P(("ctx", "tp"), None),
    )
    return jax.shard_map(
        per_device,
        mesh=mesh,
        in_specs=placed,
        out_specs=(P(("ctx", "tp"), None), P("ctx", "tp"), P("tp", None), P("tp", None), P("tp")),
        check_vma=False,
    )
```

```python
import functools
import math

import jax
import jax.numpy as jnp
from jax import lax
from jax.experimental import pallas as pl
from jax.experimental.pallas import tpu as pltpu
from jax.sharding import PartitionSpec as P

F32 = jnp.float32
BF16 = jnp.bfloat16
STEP = 8
LOCAL_FLOPS = 1_000_000_000
CLEAR_FLOPS = 4_000_000_000
PARTS_OF_WIDTH = (5, 3)


def call(body, outs, scratch, args, flops=1024, place=pltpu.VMEM):
    whole = pl.BlockSpec(memory_space=pltpu.VMEM)
    return pl.pallas_call(
        body,
        out_shape=outs,
        in_specs=[whole] * len(args),
        out_specs=[pl.BlockSpec(memory_space=place)] * len(outs),
        scratch_shapes=scratch,
        compiler_params=pltpu.CompilerParams(vmem_limit_bytes=12 << 20),
        cost_estimate=pl.CostEstimate(flops=flops, bytes_accessed=1024, transcendentals=0),
    )(*args)


def row_of(ref, at, like):
    return jnp.broadcast_to(ref[pl.ds(at, 1), :], like.shape)


def part_of(ref, which, modes):
    return ref[pl.ds(which * modes, modes), :]


def clear_body(state_ref):
    state_ref[...] = jnp.zeros_like(state_ref)


def ends_body(seq, x_ref, log_ref, zero_ref, x_f, rate_ref, ends_ref):
    tok = x_ref.shape[0]
    modes = log_ref.shape[0]
    rate = jnp.exp(log_ref[...]) / seq
    a = jnp.exp(-rate)
    rate_ref[...] = rate
    x_f[...] = x_ref[...].astype(F32)

    def steps(block, carry):
        h, q = carry
        for inner in range(STEP):
            ah = a * h
            q = a * q + ah
            h = ah + row_of(x_f, block * STEP + inner, a)
        return h, q

    h, q = lax.fori_loop(0, tok // STEP, steps, (zero_ref[...], zero_ref[...]))
    ends_ref[pl.ds(0, modes), :] = h
    ends_ref[pl.ds(modes, modes), :] = q


def table_body(rate_ref, res_ref, skip_ref, table_ref):
    modes = rate_ref.shape[0]
    rate = rate_ref[...]
    norm = jnp.sqrt(2.0 * rate)
    table_ref[pl.ds(0, modes), :] = rate
    table_ref[pl.ds(modes, modes), :] = norm
    table_ref[pl.ds(2 * modes, modes), :] = res_ref[...] * norm
    table_ref[pl.ds(3 * modes, 8), :] = jnp.broadcast_to(skip_ref[...], (8, rate.shape[1]))


def advance(h, q, a_span, span):
    return a_span * h, a_span * (q + span * h)


def pair_ends_body(tok, modes, rate_ref, own_ref, other_ref, pair_ref):
    second = lax.axis_index("ctx") % 2 == 1
    a_chunk = jnp.exp(-(rate_ref[...] * tok))
    own = part_of(own_ref, 0, modes), part_of(own_ref, 1, modes)
    other = part_of(other_ref, 0, modes), part_of(other_ref, 1, modes)
    early = [jnp.where(second, theirs, ours) for ours, theirs in zip(own, other)]
    late = [jnp.where(second, ours, theirs) for ours, theirs in zip(own, other)]
    h, q = advance(*early, a_chunk, tok)
    pair_ref[pl.ds(0, modes), :] = (h + late[0]).astype(BF16)
    pair_ref[pl.ds(modes, modes), :] = (q + late[1]).astype(BF16)


def merged_body(modes, x_f, table_ref, other_ref, *refs):
    *far_refs, merged_ref, start_ref, y_f = refs
    tok = x_f.shape[0]
    rate = part_of(table_ref, 0, modes)
    c = part_of(table_ref, 2, modes)
    a = jnp.exp(-rate)
    a_chunk = jnp.exp(-(rate * tok))
    index = lax.axis_index("ctx")
    pair = index // 2
    second = index % 2 == 1
    h = jnp.zeros_like(a)
    q = jnp.zeros_like(a)
    both = [chosen_from(far_refs, second, pl.ds(at * modes, modes)) for at in range(2)]
    for j, (far_h, far_q) in enumerate(zip(*both), 1):
        apart = pair - (pair ^ j)
        since = (jnp.maximum(apart - 1, 0) * (2 * tok)).astype(F32)
        far_h, far_q = advance(far_h, far_q, jnp.exp(-(rate * since)), since)
        h = h + jnp.where(apart > 0, far_h, 0.0)
        q = q + jnp.where(apart > 0, far_q, 0.0)
    h_late, q_late = advance(h, q, a_chunk, tok)
    h = jnp.where(second, h_late + part_of(other_ref, 0, modes), h)
    q = jnp.where(second, q_late + part_of(other_ref, 1, modes), q)
    start_ref[pl.ds(0, modes), :] = h
    start_ref[pl.ds(modes, modes), :] = q

    def steps(block, h):
        for inner in range(STEP):
            at = block * STEP + inner
            h = a * h + row_of(x_f, at, a)
            y_f[pl.ds(at, 1), :] = jnp.sum(c * h, axis=0, keepdims=True)
        return h

    lax.fori_loop(0, tok // STEP, steps, h)
    merged_ref[...] = (y_f[...] + table_ref[pl.ds(3 * modes, 1), :] * x_f[...]).astype(BF16)


def states_body(modes, x_f, table_ref, start_ref, h_ref, q_ref):
    tok = x_f.shape[0]
    a = jnp.exp(-part_of(table_ref, 0, modes))

    def steps(block, carry):
        h, q = carry
        for inner in range(STEP):
            at = block * STEP + inner
            ah = a * h
            q = a * q + ah
            h = ah + row_of(x_f, at, a)
            to = pl.ds(pl.multiple_of(at * modes, 8), modes)
            h_ref[to, :] = h
            q_ref[to, :] = q
        return h, q

    lax.fori_loop(0, tok // STEP, steps, (part_of(start_ref, 0, modes), part_of(start_ref, 1, modes)))


def grads_body(modes, rows, places_of, x_f, table_ref, h_ref, q_ref, *refs):
    *g_refs, g_f, sums_ref = refs
    tok = x_f.shape[0]
    rate = part_of(table_ref, 0, modes)
    a = jnp.exp(-rate)
    places = places_of()
    slot = 0
    for g_ref in g_refs:
        for at in range(g_ref.shape[0] // rows):
            to = pl.multiple_of(places[slot] * rows, 8)
            g_f[pl.ds(to, rows), :] = g_ref[pl.ds(at * rows, rows), :].astype(BF16).astype(F32)
            slot += 1

    def steps(block, carry):
        power, back, by_res, by_rate = carry
        for inner in range(STEP):
            at = block * STEP + inner
            g = row_of(g_f, at, a)
            to = pl.ds(pl.multiple_of(at * modes, 8), modes)
            back = back + power * g
            power = power * a
            by_res = by_res + g * h_ref[to, :]
            by_rate = by_rate + g * q_ref[to, :]
        return power, back, by_res, by_rate

    zero = jnp.zeros_like(a)
    _, back, by_res, by_rate = lax.fori_loop(0, tok // STEP, steps, (jnp.ones_like(a), zero, zero, zero))
    sums_ref[pl.ds(0, modes), :] = back
    sums_ref[pl.ds(modes, modes), :] = by_res
    sums_ref[pl.ds(2 * modes, modes), :] = 0.5 * by_res - rate * by_rate
    direct = jnp.sum(g_f[...] * x_f[...], axis=0, keepdims=True)
    sums_ref[pl.ds(3 * modes, 8), :] = jnp.broadcast_to(direct, (8, direct.shape[1]))


def pair_sums_body(tok, modes, table_ref, own_ref, other_ref, pair_ref):
    second = lax.axis_index("ctx") % 2 == 1
    a_chunk = jnp.exp(-(part_of(table_ref, 0, modes) * tok))
    own = part_of(own_ref, 0, modes)
    other = part_of(other_ref, 0, modes)
    early = jnp.where(second, other, own)
    late = jnp.where(second, own, other)
    pair_ref[pl.ds(0, modes), :] = (early + a_chunk * late).astype(BF16)
    both = pl.ds(modes, 2 * modes)
    pair_ref[both, :] = (own_ref[both, :] + other_ref[both, :]).astype(BF16)
    direct = own_ref[pl.ds(3 * modes, 1), :] + other_ref[pl.ds(3 * modes, 1), :]
    pair_ref[pl.ds(3 * modes, modes), :] = jnp.broadcast_to(direct, own.shape).astype(BF16)


def local_body(modes, g_f, table_ref, y_f, powers_ref):
    tok = g_f.shape[0]
    ahead = 8 - lax.broadcasted_iota(jnp.int32, (8, g_f.shape[1]), 0)
    for mode in range(modes):
        rate = jnp.broadcast_to(table_ref[pl.ds(mode, 1), :], ahead.shape)
        powers_ref[pl.ds(8 * mode, 8), :] = jnp.exp(-(rate * ahead.astype(F32)))
    c = part_of(table_ref, 2, modes)
    a = jnp.exp(-part_of(table_ref, 0, modes))

    def steps(block, z):
        for inner in range(STEP):
            at = tok - 1 - (block * STEP + inner)
            z = a * z + row_of(g_f, at, a)
            y_f[pl.ds(at, 1), :] = jnp.sum(c * z, axis=0, keepdims=True)
        return z

    lax.fori_loop(0, tok // STEP, steps, jnp.zeros_like(a))
    y_f[...] = y_f[...] + table_ref[pl.ds(3 * modes, 1), :] * g_f[...]


def input_body(seq, modes, own_f, powers_ref, table_ref, other_ref, pair_ref, *refs):
    *far_refs, grad_ref, by_res_ref, by_log_ref, by_skip_ref, y_f, w_ref = refs
    tok = own_f.shape[0]
    rate = part_of(table_ref, 0, modes)
    norm = part_of(table_ref, 1, modes)
    c = part_of(table_ref, 2, modes)
    a_chunk = jnp.exp(-(rate * tok))
    a_block = jnp.exp(-(rate * 8.0))
    index = lax.axis_index("ctx")
    pair = index // 2
    second = index % 2 == 1
    z = jnp.zeros_like(rate)
    for j, far_z in enumerate(chosen_from(far_refs, second, pl.ds(0, modes)), 1):
        apart = (pair ^ j) - pair
        until = (jnp.maximum(apart - 1, 0) * (2 * tok)).astype(F32)
        z = z + jnp.where(apart > 0, jnp.exp(-(rate * until)) * far_z, 0.0)
    z = jnp.where(index % 2 == 0, a_chunk * z + part_of(other_ref, 0, modes), z)

    w_ref[...] = c * z

    def steps(block, carry):
        total = None
        for mode in range(modes):
            part = row_of(w_ref, mode, powers_ref[pl.ds(0, 8), :]) * powers_ref[pl.ds(8 * mode, 8), :]
            total = part if total is None else total + part
        y_f[pl.ds(pl.multiple_of(tok - 8 * (block + 1), 8), 8), :] = total
        w_ref[...] = a_block * w_ref[...]
        return carry

    lax.fori_loop(0, tok // 8, steps, 0)
    grad_ref[...] = (own_f[...] + y_f[...]).astype(BF16)
    rest = pl.ds(modes, 3 * modes)
    total = pair_ref[rest, :].astype(F32)
    for far in chosen_from(far_refs, second, rest):
        total = total + far
    scale = 1.0 / math.sqrt(seq)
    by_res_ref[...] = scale * (norm * total[:modes])
    by_log_ref[...] = scale * (c * total[modes:2 * modes])
    by_skip_ref[...] = scale * total[2 * modes:2 * modes + 1]


def from_other_core(array, blocks):
    return lax.ppermute(array, "ctx", [(i, i ^ 1) for i in range(blocks)])


def from_pairs(array, blocks):
    if blocks != 8:
        return [lax.ppermute(array, "ctx", [(i, i ^ (2 * j)) for i in range(blocks)]) for j in range(1, blocks // 2)]
    side = lax.ppermute(array, "ctx", [(i, i ^ (4 if i % 2 else 2)) for i in range(blocks)])
    corner = lax.ppermute(array, "ctx", [(i, i ^ 6) for i in range(blocks)])
    return [side, from_other_core(side, blocks), corner]


def chosen_from(refs, second, at):
    if len(refs) != 3:
        return [ref[at, :].astype(F32) for ref in refs]
    mine, swapped, corner = (ref[at, :].astype(F32) for ref in refs)
    return [jnp.where(second, swapped, mine), jnp.where(second, mine, swapped), corner]


def outer(array):
    return lax.ppermute(array, "tp", [(0, 1), (1, 0), (2, 3), (3, 2)])


def inner(array):
    return lax.ppermute(array, "tp", [(1, 2), (2, 1), (0, 0), (3, 3)])


def back_dot(rows_in, weight):
    return lax.dot_general(rows_in, weight, (((1,), (1,)), ((), ())), preferred_element_type=F32)


def at_end():
    index = lax.axis_index("tp")
    return (index == 0) | (index == 3)


def inward(far):
    low = lax.axis_index("tp") < 2
    return jnp.where(low, 3, 0) if far else jnp.where(low, 2, 1)


def share_body(span, merged_ref, weight_ref, share_ref):
    cut = share_ref.shape[1]
    tile = min(cut, 512)
    merged = merged_ref[...]
    for at in range(0, cut, tile):
        weight = weight_ref[:, span.start + at:span.start + at + tile]
        share_ref[:, at:at + tile] = jnp.dot(merged, weight, preferred_element_type=F32).astype(BF16)


def share_rows(share_ref, at, rows):
    return share_ref[pl.ds(pl.multiple_of(at * rows, 16), rows), :]


def send_body(span, far, share_ref, passing_ref, out_ref):
    rows = out_ref.shape[0]
    end = at_end()

    @pl.when(end)
    def _():
        out_ref[...] = share_rows(share_ref, inward(far), rows)

    @pl.when(jnp.logical_not(end))
    def _():
        out_ref[...] = passing_ref[:, span]


def back_tiles(rows_ref, weight_ref, start):
    width = rows_ref.shape[1]
    tile = min(width, 1024)
    total = None
    for at in range(0, width, tile):
        part = back_dot(rows_ref[:, at:at + tile], weight_ref[:, start + at:start + at + tile])
        total = part if total is None else total + part
    return total


def near_body(own_ref, beside_ref, weight_ref, g_ref, rows_ref):
    rows = own_ref.shape[0]
    rows_ref[pl.ds(0, rows), :] = own_ref[...]
    rows_ref[pl.ds(rows, rows), :] = beside_ref[...]
    g_ref[...] = back_tiles(rows_ref, weight_ref, 0)


def far_body(span, second_ref, third_ref, across_ref, far_ref, weight_ref, *refs):
    *before_refs, g_ref, rows_ref = refs
    rows = second_ref.shape[0]
    end = at_end()

    @pl.when(end)
    def _():
        rows_ref[pl.ds(0, rows), :] = second_ref[...]
        rows_ref[pl.ds(rows, rows), :] = third_ref[...]

    @pl.when(jnp.logical_not(end))
    def _():
        rows_ref[pl.ds(0, rows), :] = across_ref[:, span]
        rows_ref[pl.ds(rows, rows), :] = far_ref[...]

    total = back_tiles(rows_ref, weight_ref, span.start)
    for before in before_refs:
        total = total + before[...]
    g_ref[...] = total


def add_body(far, share_ref, got_ref, out_ref):
    rows = out_ref.shape[0]
    block = share_rows(share_ref, inward(far), rows).astype(F32)
    out_ref[...] = (block + got_ref[...].astype(F32)).astype(BF16)


def add_whole_body(spans, *refs):
    *in_refs, out_ref = refs
    rows = out_ref.shape[0]
    for at, span in enumerate(spans):
        share_ref, got_ref = in_refs[2 * at:2 * at + 2]
        block = share_rows(share_ref, inward(False), rows).astype(F32)
        out_ref[:, span] = (block + got_ref[...].astype(F32)).astype(BF16)


def last_body(spans, *refs):
    *done_refs, share_ref, got_ref, out_ref = refs
    rows = share_ref.shape[0] // 4
    end = at_end()
    for done_ref, span in zip(done_refs, spans):
        out_ref[:, span] = done_ref[...]
    block = share_rows(share_ref, lax.axis_index("tp") ^ 1, rows).astype(F32)
    out_ref[:, spans[-1]] = (block + jnp.where(end, 0.0, got_ref[...].astype(F32))).astype(BF16)


def total_body(spans, *refs):
    *share_refs, last_ref, near_ref, out_far, out_ref, sems = refs
    rows = out_ref.shape[0]
    end = at_end()
    copies = []
    for at, (share_ref, span) in enumerate(zip(share_refs, spans)):
        total = share_rows(share_ref, lax.axis_index("tp"), rows).astype(F32) + last_ref[:, span].astype(F32)
        out_ref[:, span] = (total + jnp.where(end, 0.0, near_ref[:, span].astype(F32))).astype(BF16)
        copies.append(pltpu.make_async_copy(out_ref.at[:, span], out_far.at[:, span], sems.at[at]))
        copies[-1].start()
    for copy in copies:
        copy.wait()


def line_of_four(out_grad, out_weight, merged, x_f, states_of, grads_of):
    rows, width = out_grad.shape
    unit = width // sum(PARTS_OF_WIDTH)
    bounds = [sum(PARTS_OF_WIDTH[:at]) * unit for at in range(len(PARTS_OF_WIDTH) + 1)]
    spans = [slice(*pair) for pair in zip(bounds, bounds[1:])]
    cuts = [span.stop - span.start for span in spans]
    piece = [[jax.ShapeDtypeStruct((rows, cut), BF16)] for cut in cuts]
    whole = [jax.ShapeDtypeStruct((rows, width), BF16)]
    pairs_of = lambda ones, twos: [ref for pair in zip(ones, twos) for ref in pair]

    across = inner(out_grad)
    beside = outer(out_grad)

    shares = []
    second = []
    for at, span in enumerate(spans):
        (share,) = call(
            functools.partial(share_body, span), [jax.ShapeDtypeStruct((merged.shape[0], cuts[at]), BF16)], [],
            [merged, out_weight],
        )
        shares.append(share)
        (part,) = call(functools.partial(send_body, span, True), piece[at], [], [share, across])
        second.append(outer(part))
        merged = lax.optimization_barrier((merged, part))[0]
    beside = lax.optimization_barrier((beside, part))[0]
    across_far = [inner(beside[:, span]) for span in spans]
    g_rows = [jax.ShapeDtypeStruct((2 * rows, out_weight.shape[0]), F32)]
    (g_near,) = call(near_body, g_rows, [pltpu.VMEM((2 * rows, width), BF16)], [out_grad, beside, out_weight])
    second[0] = lax.optimization_barrier((second[0], g_near))[0]
    third = []
    to_far = []
    for at in range(len(spans)):
        (sent,) = call(functools.partial(add_body, True), piece[at], [], [shares[at], second[at]])
        to_far.append(inner(sent))
        far = lax.optimization_barrier((across_far[at], sent))[0]
        (sent,) = call(functools.partial(send_body, slice(None), False), piece[at], [], [shares[at], far])
        third.append(outer(sent))
        if at + 1 < len(spans):
            states = states_of(lax.optimization_barrier((x_f, sent))[0])
            second[at + 1] = lax.optimization_barrier((second[at + 1], *states))[0]
    g_far = []
    ready = []
    for at, span in enumerate(spans):
        g_far = call(
            functools.partial(far_body, span), g_rows, [pltpu.VMEM((2 * rows, cuts[at]), BF16)],
            [second[at], third[at], across, across_far[at], out_weight, *g_far],
        )
        if at == 0:
            got = lax.optimization_barrier((to_far[0], *g_far))[0]
            ready = call(functools.partial(last_body, [slice(None)]), piece[0], [], [shares[0], got])
            third[-1] = lax.optimization_barrier((third[-1], *ready))[0]
    ready = call(functools.partial(last_body, spans), whole, [], [*ready, shares[-1], to_far[-1]])[0]
    (near,) = call(functools.partial(add_whole_body, spans), whole, [], pairs_of(shares, third))
    ready, near, *g_far = lax.optimization_barrier((ready, near, *g_far))

    def places():
        at = lax.axis_index("tp")
        return [at, at ^ 1, inward(False), inward(True)]

    g_f, sums = grads_of([g_near, *g_far], places, states)
    last = outer(ready)
    to_near = inner(near)
    (out,) = call(
        functools.partial(total_body, spans), whole,
        [pltpu.VMEM((rows, width), BF16), pltpu.SemaphoreType.DMA((len(spans),))],
        [*shares, last, to_near], place=pl.ANY,
    )
    return out, g_f, sums


def any_axis(out_grad, out_weight, merged, x_f, states_of, grads_of):
    parts = lax.axis_size("tp")
    gathered = lax.all_gather(out_grad, "tp", axis=0, tiled=True)
    share = jnp.dot(merged, out_weight, preferred_element_type=F32).astype(BF16)
    out = lax.psum_scatter(share, "tp", scatter_dimension=0, tiled=True)
    return out, *grads_of([back_dot(gathered, out_weight)], lambda: list(range(parts)), states_of(x_f))


def per_device(inputs, residue, log_rate, skip, out_weight, out_grad):
    blocks = lax.axis_size("ctx")
    parts = lax.axis_size("tp")
    tok, chans = inputs.shape
    seq = blocks * tok
    rows = out_grad.shape[0]
    modes = residue.shape[1]
    lanes = functools.partial(jax.ShapeDtypeStruct, dtype=F32)
    state = lanes((modes, chans))
    token_f = pltpu.VMEM((tok, chans), F32)

    x_f, rate, ends = call(
        functools.partial(ends_body, seq), [lanes((tok, chans)), state, lanes((2 * modes, chans))], [],
        [inputs, log_rate.T, *call(clear_body, [state], [], [], flops=CLEAR_FLOPS)], flops=2_000_000_000,
    )
    (table,) = call(
        table_body, [lanes((3 * modes + 8, chans))], [], [rate, residue.T, skip[None, :]], flops=1_000_000_000
    )
    other_ends = from_other_core(ends, blocks)
    (pair_ends,) = call(
        functools.partial(pair_ends_body, tok, modes), [jax.ShapeDtypeStruct((2 * modes, chans), BF16)], [],
        [rate, ends, other_ends],
    )
    merged, start = call(
        functools.partial(merged_body, modes),
        [jax.ShapeDtypeStruct((tok, chans), BF16), lanes((2 * modes, chans))],
        [token_f], [x_f, table, other_ends, *from_pairs(pair_ends, blocks)],
    )

    def states_of(x_f):
        return call(
            functools.partial(states_body, modes), [lanes((tok * modes, chans))] * 2, [], [x_f, table, start]
        )

    def grads_of(pieces, places, states):
        return call(
            functools.partial(grads_body, modes, rows, places), [lanes((tok, chans)), lanes((3 * modes + 8, chans))], [],
            [x_f, table, *states, *pieces],
        )

    reduce = line_of_four if parts == 4 else any_axis
    out, g_f, sums = reduce(out_grad, out_weight, merged, x_f, states_of, grads_of)
    own_grad, powers = call(
        functools.partial(local_body, modes), [lanes((tok, chans)), lanes((8 * modes, chans))], [], [g_f, table],
        flops=LOCAL_FLOPS,
    )
    other_sums = from_other_core(sums, blocks)
    (pair_sums,) = call(
        functools.partial(pair_sums_body, tok, modes), [jax.ShapeDtypeStruct((4 * modes, chans), BF16)], [],
        [table, sums, other_sums],
    )
    grad_input, by_res, by_log, by_skip = call(
        functools.partial(input_body, seq, modes),
        [jax.ShapeDtypeStruct((tok, chans), BF16), state, state, lanes((1, chans))], [token_f, pltpu.VMEM((modes, chans), F32)],
        [own_grad, powers, table, other_sums, pair_sums, *from_pairs(pair_sums, blocks)],
    )
    return out, grad_input, by_res.T, by_log.T, by_skip[0]


def solution(mesh):
    placed = (
        P("ctx", "tp"),
        P("tp", None),
        P("tp", None),
        P("tp"),
        P("tp", None),
        P(("ctx", "tp"), None),
    )
    return jax.shard_map(
        per_device,
        mesh=mesh,
        in_specs=placed,
        out_specs=(P(("ctx", "tp"), None), P("ctx", "tp"), P("tp", None), P("tp", None), P("tp")),
        check_vma=False,
    )
```
